128 devices in a mesh: seq: 16 (over x_hi, y, core), head: 8 (over x_lo, z).
Axes of the slice: x: 4 (x_hi: 2, x_lo: 2; x = x_hi * 2 + x_lo), y: 4, z: 4, core: 2. Of those that a mesh axis runs over, the one named last changes fastest.
Arguments:
- lightning_qkv: bfloat16 [8192, 3, 4096], P('seq', None, 'head'), may hold values from -1.796875 to 1.796875
- residual: bfloat16 [8192, 6144], P(('seq', 'head')), may hold values from -6 to 6
- decay_rate: float32 [32], replicated, may hold values from 0 to 1
- lightning_gain: float32 [4096], P('head'), may hold values from 0.1 to 1.9
- out_weight: bfloat16 [4096, 6144], P('head'), may hold values from -0.09375 to 0.09375
- attn_gain: float32 [6144], replicated, may hold values from 0.1 to 1.9
- query_weight: bfloat16 [6144, 4096], P(None, 'head'), may hold values from -3 to 3
- key_value_weight: bfloat16 [6144, 8, 2, 128], P(None, 'head'), may hold values from -1 to 1
- window: int32 [32], replicated, may hold values from 512 to 1024, as said below
Outputs:
- updated: float32 [8192, 6144], P(('seq', 'head'))
- attention: bfloat16 [8192, 4096], P('seq', 'head')
The draws below stay inside these ranges and needn't reach their ends.
Inputs may be any that keep to these rules, and one draw needn't show every extreme that they name: Query head h at position i sees keys at positions i - window[h] + 1 to i.
All inputs are finite; a program needn't handle non-finite values.
Results may differ from the reference program's by a relative error of at most 0.03.
Values may be sent and summed in bfloat16 or wider, within the bound.
A program may use at most 128 MiB of HBM per device.

```python
import math
import jax
import jax.numpy as jnp
from jax import lax

MODEL_WIDTH = 6144
HL = 32
QUERY_HEADS = 32
KEY_VALUE_HEADS = 8
HEAD_SIZE = 128
TOKENS_PER_SHARD = 512
TOKEN_COUNT = 8192
WIN = 1024
N_HEAD = 8


def draw_decay_rate(key, part):
    order = jax.random.permutation(jax.random.fold_in(key, 1), HL)
    spread = jax.random.uniform(jax.random.fold_in(key, 2), (HL,), jnp.float32)
    slow = jnp.exp(math.log(0.05 / TOKEN_COUNT) + spread * math.log(46.0))
    fast = jnp.exp(math.log(0.02) + spread * math.log(4.0))
    quick = order < HL // 2
    return jnp.where(quick, fast, slow).astype(jnp.float32)


def attention_weights(key):
    key_value_piece = jnp.clip(jax.random.normal(jax.random.fold_in(key, 11), (MODEL_WIDTH, KEY_VALUE_HEADS, 2, HEAD_SIZE), jnp.float32), -5.0, 5.0) * MODEL_WIDTH ** (-0.5)
    query_part = jnp.clip(jax.random.normal(jax.random.fold_in(key, 12), (MODEL_WIDTH, QUERY_HEADS, HEAD_SIZE), jnp.float32), -5.0, 5.0) * MODEL_WIDTH ** (-0.5)
    return (query_part.reshape(MODEL_WIDTH, QUERY_HEADS * HEAD_SIZE), key_value_piece)


def draw_query_weight(key, part):
    query_part, key_value_piece = attention_weights(key)
    return query_part.astype(jnp.bfloat16)


def draw_key_value_weight(key, part):
    query_part, key_value_piece = attention_weights(key)
    return key_value_piece.astype(jnp.bfloat16)


def draw_window(key, part):
    values = jax.random.randint(jax.random.fold_in(key, 1), (QUERY_HEADS,), WIN // 2, WIN + 1)
    order = jax.random.permutation(jax.random.fold_in(key, 2), QUERY_HEADS)
    heads = jnp.arange(QUERY_HEADS)
    values = jnp.where(heads == order[0], WIN, values)
    values = jnp.where(heads == order[1], WIN // 2, values)
    return values.astype(jnp.int32)


def steps_of(stream_key, extent, split, least, largest):
    gain, own = 1.0, jax.random.fold_in(stream_key, 6)
    for position, shards_of in split:
        steps = jnp.exp(jax.random.uniform(jax.random.fold_in(own, position), (shards_of,), jnp.float32, least / len(split), largest / len(split)))
        gain = gain * jnp.repeat(steps, extent[position] // shards_of).reshape([-1 if axis == position else 1 for axis in range(len(extent))])
    return gain


def bell_draw(rng, shape, scale, most, shards=(), kind=jnp.bfloat16):
    result = jax.random.normal(rng, shape, jnp.float32) * scale
    if len(shards) > 0:
        result = steps_of(rng, shape, shards, -0.22, 0.18) * result
    return jnp.clip(result, min=-most, max=most).astype(kind)


def setup_inputs(seed: int = 0) -> dict:
    key_list = jax.random.split(jax.random.key(seed), 10)
    lightning_qkv = bell_draw(key_list[0], (TOKEN_COUNT, 3, HL * HEAD_SIZE), 0.3, 1.796875, ((0, 16), (2, 8)))
    residual = bell_draw(key_list[1], (TOKEN_COUNT, MODEL_WIDTH), 1.0, 6.0, ((0, 128),))
    decay_rate = draw_decay_rate(jax.random.fold_in(key_list[9], 71), 0)
    lightning_gain = jnp.clip(1.0 + 0.18 * jax.random.normal(key_list[3], (HL * HEAD_SIZE,), jnp.float32), 0.1, 1.9)
    out_weight = bell_draw(key_list[4], (HL * HEAD_SIZE, MODEL_WIDTH), (HL * HEAD_SIZE) ** -0.5, 0.09375, ((0, 8),))
    attn_gain = jnp.clip(1.0 + 0.18 * jax.random.normal(key_list[5], (MODEL_WIDTH,), jnp.float32), 0.1, 1.9)
    query_weight = draw_query_weight(jax.random.fold_in(key_list[9], 71), 0)
    key_value_weight = draw_key_value_weight(jax.random.fold_in(key_list[9], 71), 0)
    window = draw_window(jax.random.fold_in(key_list[9], 71), 0)
    return dict(lightning_qkv=lightning_qkv, residual=residual, decay_rate=decay_rate, lightning_gain=lightning_gain, out_weight=out_weight, attn_gain=attn_gain, query_weight=query_weight, key_value_weight=key_value_weight, window=window)


epsilon = 1e-06

def rms_scale(values, gain_vec):
    return values * lax.rsqrt(lax.optimization_barrier(jnp.mean(values * values, axis=-1, keepdims=True)) + epsilon) * gain_vec

def reference(lightning_qkv, residual, decay_rate, lightning_gain, out_weight, attn_gain, query_weight, key_value_weight, window):
    block_count = TOKEN_COUNT // TOKENS_PER_SHARD
    stacked = lightning_qkv.reshape(block_count, TOKENS_PER_SHARD, 3, HL, HEAD_SIZE)
    offsets = jnp.arange(TOKENS_PER_SHARD)
    spacing = (offsets[:, None] - offsets[None, :]).astype(jnp.float32)
    causal = offsets[:, None] >= offsets[None, :]
    decays = decay_rate.astype(jnp.float32)
    intra_decay = jnp.where(causal[None], jnp.exp(-decays[:, None, None] * jnp.maximum(spacing, 0.0)[None]), 0.0)
    key_decay = jnp.exp(-decays[None, :] * (TOKENS_PER_SHARD - 1 - offsets).astype(jnp.float32)[:, None])
    query_decay = jnp.exp(-decays[None, :] * (offsets + 1).astype(jnp.float32)[:, None])
    block_decay = jnp.exp(-decays * TOKENS_PER_SHARD)

    def advance(states, block_inputs):
        lin_query = block_inputs[:, 0]
        lin_key = block_inputs[:, 1]
        lin_value = block_inputs[:, 2]
        scores = jnp.einsum('ihd,jhd->hij', lin_query.astype(jnp.float32), lin_key.astype(jnp.float32))
        weights = (scores * intra_decay).astype(jnp.bfloat16)
        intra_out = jnp.einsum('hij,jhd->ihd', weights.astype(jnp.float32), lin_value.astype(jnp.float32))
        carried = jnp.einsum('ihd,hde->ihe', lin_query.astype(jnp.float32) * query_decay[:, :, None], states, precision=lax.Precision.HIGHEST)
        decayed = (lin_key.astype(jnp.float32) * key_decay[:, :, None]).astype(jnp.bfloat16)
        block_state = jnp.einsum('jhd,jhe->hde', decayed.astype(jnp.float32), lin_value.astype(jnp.float32))
        new_states = block_decay[:, None, None] * states + block_state
        return (new_states, intra_out + carried)
    _, lightning_out = lax.scan(advance, jnp.zeros((HL, HEAD_SIZE, HEAD_SIZE), jnp.float32), stacked)
    lightning_out = lightning_out.reshape(TOKEN_COUNT, HL, HEAD_SIZE)
    normed = rms_scale(lightning_out, lightning_gain.reshape(HL, HEAD_SIZE)).astype(jnp.bfloat16).reshape(TOKEN_COUNT, HL * HEAD_SIZE)
    group_width = HL * HEAD_SIZE // N_HEAD
    totals = residual.astype(jnp.float32)
    for group_id in range(N_HEAD):
        partial_value = jnp.dot(normed[:, group_id * group_width:(group_id + 1) * group_width], out_weight[group_id * group_width:(group_id + 1) * group_width], preferred_element_type=jnp.float32).astype(jnp.bfloat16)
        totals = totals + partial_value.astype(jnp.float32)
    updated = totals
    prepared_inputs = rms_scale(updated, attn_gain).astype(jnp.bfloat16)
    queries = jnp.dot(prepared_inputs, query_weight, preferred_element_type=jnp.float32).astype(jnp.bfloat16)
    key_value_rows = jnp.dot(prepared_inputs, key_value_weight.reshape(MODEL_WIDTH, KEY_VALUE_HEADS * 2 * HEAD_SIZE), preferred_element_type=jnp.float32).astype(jnp.bfloat16).reshape(TOKEN_COUNT, KEY_VALUE_HEADS, 2, HEAD_SIZE)
    padded_rows = jnp.concatenate((jnp.zeros((2 * TOKENS_PER_SHARD, KEY_VALUE_HEADS, 2, HEAD_SIZE), jnp.bfloat16), key_value_rows), axis=0)
    query_group_count = QUERY_HEADS // KEY_VALUE_HEADS
    window_reach_length = window.reshape(KEY_VALUE_HEADS, query_group_count)
    key_index = jnp.arange(3 * TOKENS_PER_SHARD)
    relative = key_index[None, :] - 2 * TOKENS_PER_SHARD - offsets[:, None]

    def attend(block_id):
        query_block = lax.dynamic_slice_in_dim(queries, (block_id * TOKENS_PER_SHARD).astype(jnp.int32), TOKENS_PER_SHARD, 0)
        query_block = query_block.reshape(TOKENS_PER_SHARD, KEY_VALUE_HEADS, query_group_count, HEAD_SIZE)
        keys_blk = lax.dynamic_slice_in_dim(padded_rows, (block_id * TOKENS_PER_SHARD).astype(jnp.int32), 3 * TOKENS_PER_SHARD, 0)
        scores = jnp.einsum('ikgd,jkd->kgij', query_block.astype(jnp.float32), keys_blk[:, :, 0].astype(jnp.float32)) * HEAD_SIZE ** (-0.5)
        key_pos = block_id * TOKENS_PER_SHARD - 2 * TOKENS_PER_SHARD + key_index
        visible = (relative[None, None] <= 0) & (relative[None, None] > -window_reach_length[:, :, None, None])
        visible = visible & (key_pos >= 0)[None, None, None, :]
        masked = jnp.where(visible, scores, -1e+30)
        row_max = lax.optimization_barrier(jnp.max(masked, axis=-1, keepdims=True))
        probs = jnp.where(visible, jnp.exp(masked - row_max), 0.0)
        totals_row = lax.optimization_barrier(jnp.sum(probs, axis=-1))
        probs_bf = probs.astype(jnp.bfloat16)
        context = jnp.einsum('kgij,jkd->ikgd', probs_bf.astype(jnp.float32), keys_blk[:, :, 1].astype(jnp.float32))
        context = context / jnp.transpose(totals_row, (2, 0, 1))[..., None]
        return context.astype(jnp.bfloat16).reshape(TOKENS_PER_SHARD, QUERY_HEADS * HEAD_SIZE)
    attention = lax.map(attend, jnp.arange(block_count, dtype=jnp.int32)).reshape(TOKEN_COUNT, QUERY_HEADS * HEAD_SIZE)
    return (updated, attention)
```

```python
import functools

import jax
import jax.numpy as jnp
from jax import lax
from jax.experimental import pallas as pl
from jax.experimental.pallas import tpu as pltpu
from jax.sharding import PartitionSpec as P

MESH = pl.DeviceIdType.MESH
F32 = jnp.float32
BF16 = jnp.bfloat16
HEAD = 128
EPS = 1e-06
TOK = 512
MODEL = 6144
NCH = 4
CH = MODEL // NCH
HALF = CH // 2
NP = 2
R = 64 // NP
QKV = 768


def coords():
    s, h = lax.axis_index("seq"), lax.axis_index("head")
    return lax.div(s, 8), lax.rem(lax.div(s, 2), 4), lax.rem(s, 2), lax.div(h, 4), lax.rem(h, 4)


def place(x, y, c, z):
    x, y, z = lax.rem(x + 4, 4), lax.rem(y + 4, 4), lax.rem(z + 4, 4)
    return (lax.div(x, 2) * 8 + y * 2 + c, lax.rem(x, 2) * 4 + z)


def dot(a, b):
    return jnp.dot(a, b, preferred_element_type=F32)


def dot_t(a, b):
    return lax.dot_general(a, b, (((1,), (1,)), ((), ())), preferred_element_type=F32)


def rows_of(shape):
    return lax.broadcasted_iota(jnp.int32, shape, 0)


def cols_of(shape):
    return lax.broadcasted_iota(jnp.int32, shape, 1)


def body(
    qkv,
    residual,
    decay,
    lgain,
    wo_hbm,
    again,
    wq_hbm,
    wkv_hbm,
    window,
    upd_out,
    att_out,
    wo_own,
    wo_par,
    wq_own,
    wq_par,
    s_own,
    s_pair,
    t_send,
    t_recv,
    p_all,
    intra,
    normed,
    nrecv,
    part,
    a_p,
    a_m,
    b_p,
    b_m,
    upd,
    gath,
    acc,
    qbuf,
    kvbuf,
    stq,
    stkv,
    own_sem,
    w_s,
    w_r,
    sp_s,
    sp_r,
    t_s,
    t_r,
    n_s,
    n_r,
    a_s,
    a_r,
    b_s,
    b_r,
    g_s,
    g_r,
    x_s,
    x_r,
    h_s,
    h_r,
):
    xh, y, c, xl, z = coords()
    x = 2 * xh + xl
    s, h = lax.axis_index("seq"), lax.axis_index("head")
    other = lax.rem(h + 4, 8)
    m = xh * 4 + y
    e = lax.rem(y, 2)
    z_up, z_dn = lax.rem(z + 1, 4), lax.rem(z + 3, 4)
    z_far = lax.rem(z + 2, 4)
    to_zu, to_zd = place(x, y, c, z + 1), place(x, y, c, z - 1)
    to_xu, to_xd = place(x + 1, y, c, z), place(x - 1, y, c, z)
    to_yu, to_yd = place(x, y + 1, c, z), place(x, y - 1, c, z)
    to_core = (s + 1 - 2 * c, h)
    to_pair = (s, other)
    sent = []

    def send(src, dst, ssem, rsem, target, later=True):
        cp = pltpu.make_async_remote_copy(
            src_ref=src, dst_ref=dst, send_sem=ssem, recv_sem=rsem,
            device_id=target, device_id_type=MESH,
        )
        cp.start()
        if later:
            sent.append(cp)
        return cp

    def arrived(dst, sem):
        pltpu.make_async_copy(dst, dst, sem).wait()

    bar = pltpu.get_barrier_semaphore()
    peers = [to_zu, to_zd, to_xu, to_xd, to_core]
    for k in range(1, 8):
        mm = lax.rem(m + k, 8)
        peers.append((mm * 2 + c, h))
    for step in (1, 2, 14, 15):
        there = lax.rem(s + step, 16)
        peers += [(there, h), (there, other)]
    for p in peers:
        pl.semaphore_signal(bar, 1, device_id=p, device_id_type=MESH)
    pl.semaphore_wait(bar, len(peers))

    own = [
        pltpu.make_async_copy(wo_hbm, wo_own, own_sem.at[0]),
        pltpu.make_async_copy(wq_hbm, wq_own.at[:, pl.ds(0, 512)], own_sem.at[1]),
        pltpu.make_async_copy(wkv_hbm, wq_own.at[:, pl.ds(512, 256)], own_sem.at[2]),
    ]

    hbm_of = (wo_hbm, wq_hbm, wkv_hbm)

    def region(a, k, cc, first, count, hbm=False):
        if a == 0:
            rows = pl.ds(pl.multiple_of(cc * 256 + first * 64, 64), count * 64)
            ref = wo_hbm if hbm else wo_par
            return ref.at[rows, pl.ds(k * CH, CH)]
        rows = pl.ds(pl.multiple_of(cc * 3072 + k * 768 + first * 192, 64), count * 192)
        if hbm:
            return hbm_of[a].at[rows]
        return wq_par.at[rows, pl.ds(0, 512) if a == 1 else pl.ds(512, 256)]

    def push(a, k):
        for d, target in ((0, to_xu), (1, to_xd)):
            send(
                region(a, k, c, e * 2 + d, 1, True), region(a, k, c, e * 2 + d, 1),
                w_s.at[a, k, d], w_r.at[a, k, d], target,
            )

    def relay(a, k):
        for d, target in ((0, to_yu), (1, to_yd)):
            piece = region(a, k, c, e * 2 + d, 1)
            arrived(piece, w_r.at[a, k, d])
            send(piece, piece, w_s.at[a, k, 2 + d], w_r.at[a, k, 2 + d], target)

    def mirror(a, k):
        for d in (0, 1):
            arrived(region(a, k, c, (1 - e) * 2 + d, 1), w_r.at[a, k, 2 + d])
        piece = region(a, k, c, 0, 4)
        send(piece, piece, w_s.at[a, k, 4], w_r.at[a, k, 4], to_core)

    def ready(a, k):
        arrived(region(a, k, 1 - c, 0, 4), w_r.at[a, k, 4])

    push(0, 0)
    for cp in own:
        cp.start()

    rate = [decay[h * 4 + i] for i in range(4)]

    def head_of(i):
        return pl.ds(i * HEAD, HEAD)

    for i in range(4):
        back = (TOK - 1 - rows_of((TOK, HEAD))).astype(F32)
        keys = qkv[1, :, head_of(i)].astype(F32) * jnp.exp(-rate[i] * back)
        s_own[i] = lax.dot_general(
            keys.astype(BF16), qkv[2, :, head_of(i)], (((0,), (0,)), ((), ())),
            preferred_element_type=F32,
        )
    send(s_own, s_pair, sp_s.at[0], sp_r.at[0], to_core)

    def within(i):
        for t in range(4):
            n = HEAD * (t + 1)
            lq = qkv[0, pl.ds(t * HEAD, HEAD), head_of(i)]
            sc = dot_t(lq, qkv[1, pl.ds(0, n), head_of(i)])
            gap = (rows_of((HEAD, n)) + t * HEAD - cols_of((HEAD, n))).astype(F32)
            fade = jnp.where(gap >= 0, jnp.exp(-rate[i] * jnp.maximum(gap, 0.0)), 0.0)
            intra[pl.ds(t * HEAD, HEAD), head_of(i)] = dot(
                (sc * fade).astype(BF16), qkv[2, pl.ds(0, n), head_of(i)]
            )

    within(0)
    arrived(s_pair, sp_r.at[0])
    for i in range(2):
        hd = 2 * c + i
        dd = decay[h * 4 + hd]
        mine, theirs = s_own[hd], s_pair[hd]
        fade = jnp.exp(jnp.full((HEAD, HEAD), -dd * TOK, F32))
        first, second = jnp.where(c == 0, mine, theirs), jnp.where(c == 0, theirs, mine)
        t_send[i] = (fade * first + second).astype(BF16)
    for mm in range(1, 8):

        @pl.when(m < mm)
        def _(mm=mm):
            send(t_send, t_recv.at[m], t_s.at[mm - 1], t_r.at[m], (mm * 2 + c, h), False)

    push(0, 1)
    push(0, 2)
    within(1)
    within(2)
    within(3)
    relay(0, 0)
    for i in range(2):
        p_all[2 * c + i] = jnp.zeros((HEAD, HEAD), F32)
    for mm in range(7):

        @pl.when(mm < m)
        def _(mm=mm):
            arrived(t_recv.at[mm], t_r.at[mm])
            for i in range(2):
                dd = decay[h * 4 + 2 * c + i]
                gone = (m - 1 - mm).astype(F32) * (2.0 * TOK)
                p_all[2 * c + i] += (
                    jnp.exp(jnp.full((HEAD, HEAD), -dd * gone, F32)) * t_recv[mm, i].astype(F32)
                )

    half_p = p_all.at[pl.ds(2 * c, 2)]
    send(half_p, half_p, sp_s.at[1], sp_r.at[1], to_core)
    relay(0, 1)
    mirror(0, 0)
    arrived(p_all.at[pl.ds(2 * (1 - c), 2)], sp_r.at[1])

    def finish(lo):
        for i in range(4):
            span = pl.ds(pl.multiple_of(lo, 256), 256)
            before = p_all[i]
            fade = jnp.exp(jnp.full((HEAD, HEAD), -rate[i] * TOK, F32))
            start = jnp.where(c == 0, before, fade * before + s_pair[i])
            ahead = (rows_of((256, HEAD)) + (lo + 1)).astype(F32)
            lq = qkv[0, span, head_of(i)].astype(F32) * jnp.exp(-rate[i] * ahead)
            full = intra[span, head_of(i)] + jnp.dot(
                lq, start, preferred_element_type=F32, precision=lax.Precision.HIGHEST
            )
            scale = lax.rsqrt(jnp.mean(full * full, axis=-1, keepdims=True) + EPS)
            normed[span, head_of(i)] = (full * scale * lgain[:, head_of(i)]).astype(BF16)

    finish((1 - xl) * 256)
    give = normed.at[pl.ds(pl.multiple_of((1 - xl) * 256, 256), 256)]
    send(give, nrecv, n_s.at[0], n_r.at[0], to_pair)
    push(0, 3)
    for k in range(4):
        push(1, k)
        push(2, k)
    finish(xl * 256)
    relay(0, 2)
    mirror(0, 1)
    own[0].wait()
    arrived(nrecv, n_r.at[0])

    def block(zz):
        return pl.ds(pl.multiple_of(zz * 64, 64), 64)

    keep = pl.ds(pl.multiple_of(xl * 256, 256), 256)

    def project(k):
        ready(0, k)

        def tile(j, carry):
            at = pl.ds(pl.multiple_of(k * CH + j * 512, 512), 512)
            total = dot(normed[keep, :], wo_own[:, at]) + dot(nrecv[...], wo_par[:, at])
            part[:, at] = total.astype(BF16)
            return carry

        lax.fori_loop(0, CH // 512, tile, 0)
        left, right = pl.ds(k * CH, HALF), pl.ds(k * CH + HALF, HALF)
        slot = pl.ds(k * HALF, HALF)
        send(part.at[block(z_far), left], a_p.at[:, slot], a_s.at[k, 0], a_r.at[k, 0], to_zu)
        send(part.at[block(z_far), right], a_m.at[:, slot], a_s.at[k, 1], a_r.at[k, 1], to_zd)

    def join(k):
        left, right = pl.ds(k * CH, HALF), pl.ds(k * CH + HALF, HALF)
        slot, chunk = pl.ds(k * HALF, HALF), pl.ds(k * CH, CH)
        arrived(a_p.at[:, slot], a_r.at[k, 0])
        part[block(z_up), left] = (
            part[block(z_up), left].astype(F32) + a_p[:, slot].astype(F32)
        ).astype(BF16)
        send(part.at[block(z_up), chunk], b_p.at[:, chunk], b_s.at[k, 0], b_r.at[k, 0], to_zu)
        arrived(a_m.at[:, slot], a_r.at[k, 1])
        part[block(z_dn), right] = (
            part[block(z_dn), right].astype(F32) + a_m[:, slot].astype(F32)
        ).astype(BF16)
        send(part.at[block(z_dn), chunk], b_m.at[:, chunk], b_s.at[k, 1], b_r.at[k, 1], to_zd)

    def close(k):
        chunk = pl.ds(k * CH, CH)
        arrived(b_p.at[:, chunk], b_r.at[k, 0])
        arrived(b_m.at[:, chunk], b_r.at[k, 1])
        total = (
            residual[:, chunk].astype(F32) + part[block(z), chunk].astype(F32)
            + b_p[:, chunk].astype(F32) + b_m[:, chunk].astype(F32)
        )
        upd[:, chunk] = total
        return jnp.sum(total * total, axis=-1, keepdims=True)

    project(0)
    mirror(0, 2)
    project(1)
    join(0)
    relay(0, 3)
    project(2)
    join(1)
    mirror(0, 3)
    project(3)
    join(2)
    join(3)
    relay(1, 0)
    relay(2, 0)
    square = close(0)
    square += close(1)
    relay(1, 1)
    relay(2, 1)
    mirror(1, 0)
    mirror(2, 0)
    square += close(2)
    square += close(3)
    scale = lax.rsqrt(square * (1.0 / MODEL) + EPS)
    store = pltpu.make_async_copy(upd, upd_out, own_sem.at[3])
    store.start()

    for p in range(NP):
        row = pl.ds(p * R, R)
        gath[p, z] = (upd[row, :] * scale[p * R : (p + 1) * R] * again[...]).astype(BF16)
        mine = gath.at[p, z]
        send(mine, mine, g_s.at[p, 0], g_r.at[p, 0], to_zu)
        send(mine, mine, g_s.at[p, 1], g_r.at[p, 1], to_zd)

    def forward(p):
        below, above = gath.at[p, z_dn], gath.at[p, z_up]
        left, right = pl.ds(0, MODEL // 2), pl.ds(MODEL // 2, MODEL // 2)
        arrived(below, g_r.at[p, 0])
        send(below.at[:, left], below.at[:, left], g_s.at[p, 2], g_r.at[p, 2], to_zu)
        arrived(above, g_r.at[p, 1])
        send(above.at[:, right], above.at[:, right], g_s.at[p, 3], g_r.at[p, 3], to_zd)

    def gathered(p):
        far = gath.at[p, z_far]
        arrived(far.at[:, pl.ds(0, MODEL // 2)], g_r.at[p, 2])
        arrived(far.at[:, pl.ds(MODEL // 2, MODEL // 2)], g_r.at[p, 3])

    mine_half, mine_kv = pl.ds(xl * 4, 4), pl.ds(16 + xl * 4, 4)

    def second(p):
        acc[...] = jnp.zeros_like(acc)

        def deep(j, carry):
            at = pl.ds(pl.multiple_of(j * 1024, 1024), 1024)
            lhs = gath[p, :, :, at].reshape(4 * R, 1024)
            acc[:, pl.ds(0, QKV)] += dot(lhs, wq_own[at, :])
            acc[:, pl.ds(QKV, QKV)] += dot(lhs, wq_par[at, :])
            return carry

        lax.fori_loop(0, 6, deep, 0)
        stkv[p] = acc[:, pl.ds(QKV + 512, 256)].astype(BF16).reshape(4, R, 256)
        kvbuf[mine_kv, p] = acc[:, pl.ds(512, 256)].astype(BF16).reshape(4, R, 256)
        send(stkv.at[p], kvbuf.at[mine_kv, p], x_s.at[p, 0], x_r.at[p, 0], to_pair)
        for step in (1, 2):

            @pl.when(s + step < 16)
            def _(step=step):
                slot = kvbuf.at[pl.ds(16 - 8 * step + xl * 4, 4), p]
                sem = h_r.at[p, step - 1, xl]
                send(kvbuf.at[mine_kv, p], slot, h_s.at[p, step - 1, 0], sem, (s + step, h), False)
                send(stkv.at[p], slot, h_s.at[p, step - 1, 1], sem, (s + step, other), False)

        stq[p] = acc[:, pl.ds(QKV, 512)].astype(BF16).reshape(4, R, 512)
        send(stq.at[p], qbuf.at[mine_half, p], x_s.at[p, 1], x_r.at[p, 1], to_pair)
        qbuf[mine_half, p] = acc[:, pl.ds(0, 512)].astype(BF16).reshape(4, R, 512)

    relay(1, 2)
    relay(2, 2)
    mirror(1, 1)
    mirror(2, 1)
    forward(0)
    relay(1, 3)
    relay(2, 3)
    mirror(1, 2)
    mirror(2, 2)
    forward(1)
    mirror(1, 3)
    mirror(2, 3)
    own[1].wait()
    own[2].wait()
    for k in range(4):
        ready(1, k)
        ready(2, k)
    gathered(0)
    second(0)
    gathered(1)
    second(1)

    @pl.when(s < 1)
    def _():
        kvbuf[pl.ds(8, 8)] = jnp.zeros((8, NP, R, 256), BF16)

    @pl.when(s < 2)
    def _():
        kvbuf[pl.ds(0, 8)] = jnp.zeros((8, NP, R, 256), BF16)

    for p in range(NP):
        arrived(kvbuf.at[pl.ds(16 + (1 - xl) * 4, 4), p], x_r.at[p, 0])
        for step in (1, 2):

            @pl.when(s - step >= 0)
            def _(p=p, step=step):
                for hf in (0, 1):
                    slot = kvbuf.at[pl.ds(16 - 8 * step + hf * 4, 4), p]
                    arrived(slot, h_r.at[p, step - 1, hf])

        arrived(qbuf.at[pl.ds((1 - xl) * 4, 4), p], x_r.at[p, 1])

    def attend(t, carry):
        shape = (HEAD, 1152)
        row, col = rows_of(shape), cols_of(shape)
        gap = col - row
        early = 1024 - s * TOK - t * HEAD
        keys = kvbuf[pl.ds(2 * t, 18), :, :, pl.ds(0, HEAD)].reshape(1152, HEAD)
        vals = kvbuf[pl.ds(2 * t, 18), :, :, pl.ds(HEAD, HEAD)].reshape(1152, HEAD)
        for i in range(4):
            reach = window[h * 4 + i]
            seen = (gap <= 1024) & (gap > 1024 - reach) & (col >= early)
            q = qbuf[pl.ds(2 * t, 2), :, :, head_of(i)].reshape(HEAD, HEAD)
            sc = dot_t(q, keys) * (HEAD**-0.5)
            sc = jnp.where(seen, sc, -1e30)
            top = jnp.max(sc, axis=-1, keepdims=True)
            pr = jnp.where(seen, jnp.exp(sc - top), 0.0)
            total = jnp.sum(pr, axis=-1, keepdims=True)
            out = dot(pr.astype(BF16), vals) / total
            att_out[pl.ds(pl.multiple_of(t * HEAD, HEAD), HEAD), head_of(i)] = out.astype(BF16)
        return carry

    lax.fori_loop(0, 4, attend, 0)

    store.wait()
    for cp in sent:
        cp.wait_send()
    for mm in range(1, 8):

        @pl.when(m < mm)
        def _(mm=mm):
            pltpu.make_async_copy(t_send, t_send, t_s.at[mm - 1]).wait()

    for p in range(NP):
        for step in (1, 2):

            @pl.when(s + step < 16)
            def _(p=p, step=step):
                pltpu.make_async_copy(stkv.at[p], stkv.at[p], h_s.at[p, step - 1, 0]).wait()
                pltpu.make_async_copy(stkv.at[p], stkv.at[p], h_s.at[p, step - 1, 1]).wait()


def on_device(
    lightning_qkv,
    residual,
    decay_rate,
    lightning_gain,
    out_weight,
    attn_gain,
    query_weight,
    key_value_weight,
    window,
):
    vmem = pl.BlockSpec(memory_space=pltpu.VMEM)
    smem = pl.BlockSpec(memory_space=pltpu.SMEM)
    anyw = pl.BlockSpec(memory_space=pl.ANY)
    dma = pltpu.SemaphoreType.DMA
    V = pltpu.VMEM
    return pl.pallas_call(
        body,
        out_shape=(
            jax.ShapeDtypeStruct((64, MODEL), F32),
            jax.ShapeDtypeStruct((TOK, 512), BF16),
        ),
        in_specs=[vmem, vmem, smem, vmem, anyw, vmem, anyw, anyw, smem],
        out_specs=(anyw, vmem),
        scratch_shapes=[
            V((512, MODEL), BF16),
            V((512, MODEL), BF16),
            V((MODEL, QKV), BF16),
            V((MODEL, QKV), BF16),
            V((4, HEAD, HEAD), F32),
            V((4, HEAD, HEAD), F32),
            V((2, HEAD, HEAD), BF16),
            V((7, 2, HEAD, HEAD), BF16),
            V((4, HEAD, HEAD), F32),
            V((TOK, 512), F32),
            V((TOK, 512), BF16),
            V((256, 512), BF16),
            V((256, MODEL), BF16),
            V((64, MODEL // 2), BF16),
            V((64, MODEL // 2), BF16),
            V((64, MODEL), BF16),
            V((64, MODEL), BF16),
            V((64, MODEL), F32),
            V((NP, 4, R, MODEL), BF16),
            V((4 * R, 2 * QKV), F32),
            V((8, NP, R, 512), BF16),
            V((24, NP, R, 256), BF16),
            V((NP, 4, R, 512), BF16),
            V((NP, 4, R, 256), BF16),
            dma((4,)),
            dma((3, 4, 5)),
            dma((3, 4, 5)),
            dma((2,)),
            dma((2,)),
            dma((7,)),
            dma((7,)),
            dma((1,)),
            dma((1,)),
            dma((NCH, 2)),
            dma((NCH, 2)),
            dma((NCH, 2)),
            dma((NCH, 2)),
            dma((NP, 4)),
            dma((NP, 4)),
            dma((NP, 2)),
            dma((NP, 2)),
            dma((NP, 2, 2)),
            dma((NP, 2, 2)),
        ],
        compiler_params=pltpu.CompilerParams(
            collective_id=0, has_side_effects=True, vmem_limit_bytes=60 * 2**20
        ),
    )(
        jnp.transpose(lightning_qkv, (1, 0, 2)),
        residual,
        decay_rate,
        lightning_gain.reshape(1, 512),
        out_weight,
        attn_gain.reshape(1, MODEL),
        query_weight,
        key_value_weight.reshape(MODEL, 256),
        window,
    )


def solution(mesh):
    placed = (
        P("seq", None, "head"),
        P(("seq", "head"), None),
        P(),
        P("head"),
        P("head", None),
        P(),
        P(None, "head"),
        P(None, "head", None, None),
        P(),
    )
    return jax.shard_map(
        on_device,
        mesh=mesh,
        in_specs=placed,
        out_specs=(P(("seq", "head"), None), P("seq", "head")),
        check_vma=False,
    )
```

```python
import functools

import jax
import jax.numpy as jnp
from jax import lax
from jax.experimental import pallas as pl
from jax.experimental.pallas import tpu as pltpu
from jax.sharding import PartitionSpec as P

MESH = pl.DeviceIdType.MESH
F32 = jnp.float32
BF16 = jnp.bfloat16
HEAD = 128
EPS = 1e-06
TOK = 512
MODEL = 6144
NCH = 8
CH = MODEL // NCH
HALF = CH // 2
NP = 2
R = 64 // NP
QKV = 768


def coords():
    s, h = lax.axis_index("seq"), lax.axis_index("head")
    return lax.div(s, 8), lax.rem(lax.div(s, 2), 4), lax.rem(s, 2), lax.div(h, 4), lax.rem(h, 4)


def place(x, y, c, z):
    x, y, z = lax.rem(x + 4, 4), lax.rem(y + 4, 4), lax.rem(z + 4, 4)
    return (lax.div(x, 2) * 8 + y * 2 + c, lax.rem(x, 2) * 4 + z)


def dot(a, b):
    return jnp.dot(a, b, preferred_element_type=F32)


def dot_t(a, b):
    return lax.dot_general(a, b, (((1,), (1,)), ((), ())), preferred_element_type=F32)


def rows_of(shape):
    return lax.broadcasted_iota(jnp.int32, shape, 0)


def cols_of(shape):
    return lax.broadcasted_iota(jnp.int32, shape, 1)


def body(
    qkv,
    residual,
    decay,
    lgain,
    wo_hbm,
    again,
    wq_hbm,
    wkv_hbm,
    window,
    upd_out,
    att_out,
    wo_own,
    wo_par,
    wq_own,
    wq_par,
    wkv_own,
    wkv_par,
    wide,
    s_own,
    s_pair,
    t_send,
    t_recv,
    p_all,
    intra,
    nsend,
    nown,
    nrecv,
    part,
    a_p,
    a_m,
    b_p,
    b_m,
    upd,
    gath,
    acc,
    qbuf,
    kvbuf,
    stq,
    stkv,
    own_sem,
    w_s,
    w_r,
    sp_s,
    sp_r,
    t_s,
    t_r,
    n_s,
    n_r,
    a_s,
    a_r,
    b_s,
    b_r,
    g_s,
    g_r,
    x_s,
    x_r,
    h_s,
    h_r,
):
    xh, y, c, xl, z = coords()
    x = 2 * xh + xl
    s, h = lax.axis_index("seq"), lax.axis_index("head")
    other = lax.rem(h + 4, 8)
    m = xh * 4 + y
    e = lax.rem(y, 2)
    z_up, z_dn = lax.rem(z + 1, 4), lax.rem(z + 3, 4)
    z_far = lax.rem(z + 2, 4)
    to_zu, to_zd = place(x, y, c, z + 1), place(x, y, c, z - 1)
    to_outer = place(x + 2 * xl - 1, y, c, z)
    to_yu, to_yd = place(x, y + 1, c, z), place(x, y - 1, c, z)
    to_core = (s + 1 - 2 * c, h)
    to_pair = (s, other)
    sent = []

    def send(src, dst, ssem, rsem, target, later=True):
        cp = pltpu.make_async_remote_copy(
            src_ref=src, dst_ref=dst, send_sem=ssem, recv_sem=rsem,
            device_id=target, device_id_type=MESH,
        )
        cp.start()
        if later:
            sent.append(cp)
        return cp

    def arrived(dst, sem):
        pltpu.make_async_copy(dst, dst, sem).wait()

    bar = pltpu.get_barrier_semaphore()
    peers = [to_zu, to_zd, to_pair, to_outer, to_core]
    for k in range(1, 8):
        mm = lax.rem(m + k, 8)
        peers.append((mm * 2 + c, h))
    for step in (1, 2, 14, 15):
        there = lax.rem(s + step, 16)
        peers += [(there, h), (there, other)]
    for p in peers:
        pl.semaphore_signal(bar, 1, device_id=p, device_id_type=MESH)

    own = [
        pltpu.make_async_copy(wo_hbm, wo_own, own_sem.at[0]),
        pltpu.make_async_copy(wq_hbm, wq_own.at[:, pl.ds(0, 512)], own_sem.at[1]),
        pltpu.make_async_copy(wkv_hbm, wkv_own, own_sem.at[2]),
    ]

    hbm_of = (wo_hbm, wq_hbm, wkv_hbm)

    def region(a, k, cc, par, d, hbm=False):
        whole, cut = (128, 48) if a == 0 else (384 * a, 176 * a)
        base = cc * 256 if a == 0 else cc * 8 * whole + k * 2 * whole
        count = (cut, whole - cut, 2 * whole)[d]
        base = base + par * whole + (cut if d == 1 else 0)
        rows = pl.ds(pl.multiple_of(base, 16), count)
        if a == 0:
            return (wo_hbm if hbm else wo_par).at[rows, pl.ds(k * CH, CH)]
        if hbm:
            return hbm_of[a].at[rows]
        return wq_par.at[rows, pl.ds(0, 512)] if a == 1 else wkv_par.at[rows]

    def push(a, k, d):
        send(
            region(a, k, c, e, d, True), region(a, k, c, e, d),
            w_s.at[a, k, d], w_r.at[a, k, d], (to_pair, to_outer)[d],
        )

    def relay(a, k):
        for d in (0, 1):
            piece = region(a, k, c, e, d)
            arrived(piece, w_r.at[a, k, d])
            target = (to_yu, to_yd)[(d + k) % 2]
            send(piece, piece, w_s.at[a, k, 2 + d], w_r.at[a, k, 2 + d], target)

    def mirror(a, k):
        for d in (0, 1):
            arrived(region(a, k, c, 1 - e, d), w_r.at[a, k, 2 + d])
        piece = region(a, k, c, 0, 2)
        send(piece, piece, w_s.at[a, k, 4], w_r.at[a, k, 4], to_core)

    def ready(a, k):
        arrived(region(a, k, 1 - c, 0, 2), w_r.at[a, k, 4])

    def separate(raw, to, first, count):
        def piece(j, carry):
            at = pl.multiple_of(first + j * 384, 64)
            wide[...] = raw[pl.ds(pl.multiple_of(2 * at, 128), 768), :].astype(F32)
            for i in (0, 1):
                cols = pl.ds(512 + i * HEAD, HEAD)
                to[pl.ds(at, 384), cols] = wide[pl.ds(i, 384, stride=2), :].astype(BF16)
            return carry

        lax.fori_loop(0, count // 384, piece, 0)

    for cp in own:
        cp.start()

    rate = [decay[h * 4 + i] for i in range(4)]

    def head_of(i):
        return pl.ds(i * HEAD, HEAD)

    for i in range(4):
        back = (TOK - 1 - rows_of((TOK, HEAD))).astype(F32)
        keys = qkv[1, :, head_of(i)].astype(F32) * jnp.exp(-rate[i] * back)
        s_own[i] = lax.dot_general(
            keys.astype(BF16), qkv[2, :, head_of(i)], (((0,), (0,)), ((), ())),
            preferred_element_type=F32,
        )
    pl.semaphore_wait(bar, len(peers))
    push(0, 0, 1)
    push(0, 0, 0)
    send(s_own, s_pair, sp_s.at[0], sp_r.at[0], to_core)

    def within(i):
        for t in range(4):
            n = HEAD * (t + 1)
            lq = qkv[0, pl.ds(t * HEAD, HEAD), head_of(i)]
            sc = dot_t(lq, qkv[1, pl.ds(0, n), head_of(i)])
            gap = (rows_of((HEAD, n)) + t * HEAD - cols_of((HEAD, n))).astype(F32)
            fade = jnp.where(gap >= 0, jnp.exp(-rate[i] * jnp.maximum(gap, 0.0)), 0.0)
            intra[pl.ds(t * HEAD, HEAD), head_of(i)] = dot(
                (sc * fade).astype(BF16), qkv[2, pl.ds(0, n), head_of(i)]
            )

    within(0)
    arrived(s_pair, sp_r.at[0])
    for i in range(2):
        hd = 2 * c + i
        dd = decay[h * 4 + hd]
        mine, theirs = s_own[hd], s_pair[hd]
        fade = jnp.exp(jnp.full((HEAD, HEAD), -dd * TOK, F32))
        first, second = jnp.where(c == 0, mine, theirs), jnp.where(c == 0, theirs, mine)
        t_send[i] = (fade * first + second).astype(BF16)
    for mm in range(1, 8):

        @pl.when(m < mm)
        def _(mm=mm):
            send(t_send, t_recv.at[m], t_s.at[mm - 1], t_r.at[m], (mm * 2 + c, h), False)

    for k in range(1, NCH):
        push(0, k, 1)
    for k in range(1, 6):
        push(0, k, 0)
    for k in range(4):
        push(1, k, 1)
        push(2, k, 1)
    within(1)
    within(2)
    within(3)
    relay(0, 0)
    relay(0, 1)
    for i in range(2):
        p_all[2 * c + i] = jnp.zeros((HEAD, HEAD), F32)
    for mm in range(7):

        @pl.when(mm < m)
        def _(mm=mm):
            arrived(t_recv.at[mm], t_r.at[mm])
            for i in range(2):
                dd = decay[h * 4 + 2 * c + i]
                gone = (m - 1 - mm).astype(F32) * (2.0 * TOK)
                p_all[2 * c + i] += (
                    jnp.exp(jnp.full((HEAD, HEAD), -dd * gone, F32)) * t_recv[mm, i].astype(F32)
                )

    half_p = p_all.at[pl.ds(2 * c, 2)]
    across = send(half_p, half_p, sp_s.at[1], sp_r.at[1], to_core, False)
    relay(0, 2)
    arrived(p_all.at[pl.ds(2 * (1 - c), 2)], sp_r.at[1])

    order = (z_far, z_up, z_dn, z)

    def finish(to, lo, j):
        first = lo + order[j] * 64
        span, out = pl.ds(pl.multiple_of(first, 64), 64), pl.ds(j * 64, 64)
        for i in range(4):
            ahead = (rows_of((64, HEAD)) + (first + 1)).astype(F32)
            lq = qkv[0, span, head_of(i)].astype(F32) * jnp.exp(-rate[i] * ahead)
            full = intra[span, head_of(i)] + jnp.dot(
                lq, p_all[i], preferred_element_type=F32, precision=lax.Precision.HIGHEST
            )
            scale = lax.rsqrt(jnp.mean(full * full, axis=-1, keepdims=True) + EPS)
            to[out, head_of(i)] = (full * scale * lgain[:, head_of(i)]).astype(BF16)

    def four(j):
        return pl.ds(j * 64, 64)

    across.wait_send()

    @pl.when(c == 1)
    def _():
        for i in range(4):
            fade = jnp.exp(jnp.full((HEAD, HEAD), -rate[i] * TOK, F32))
            p_all[i] = fade * p_all[i] + s_pair[i]

    for j in range(4):
        finish(nsend, (1 - xl) * 256, j)
        send(nsend.at[four(j)], nrecv.at[four(j)], n_s.at[j], n_r.at[j], to_pair)
    push(0, 6, 0)
    push(0, 7, 0)
    for k in range(4):
        push(1, k, 0)
        push(2, k, 0)
    relay(0, 3)
    mirror(0, 0)
    for j in range(4):
        finish(nown, xl * 256, j)
    mirror(0, 1)
    relay(0, 4)
    own[0].wait()

    def project(k, lo, count):
        at, rows = pl.ds(k * CH, CH), pl.ds(lo, count)
        total = dot(nown[rows, :], wo_own[:, at]) + dot(nrecv[rows, :], wo_par[:, at])
        part[rows, at] = total.astype(BF16)

    def far(k):
        ready(0, k)
        project(k, 0, 64)
        left, right = pl.ds(k * CH, HALF), pl.ds(k * CH + HALF, HALF)
        slot = pl.ds(k * HALF, HALF)
        send(part.at[four(0), left], a_p.at[:, slot], a_s.at[k, 0], a_r.at[k, 0], to_zu)
        send(part.at[four(0), right], a_m.at[:, slot], a_s.at[k, 1], a_r.at[k, 1], to_zd)

    def join(k):
        left, right = pl.ds(k * CH, HALF), pl.ds(k * CH + HALF, HALF)
        slot, chunk = pl.ds(k * HALF, HALF), pl.ds(k * CH, CH)
        project(k, 64, 192)
        arrived(a_p.at[:, slot], a_r.at[k, 0])
        part[four(1), left] = (
            part[four(1), left].astype(F32) + a_p[:, slot].astype(F32)
        ).astype(BF16)
        send(part.at[four(1), chunk], b_p.at[:, chunk], b_s.at[k, 0], b_r.at[k, 0], to_zu)
        arrived(a_m.at[:, slot], a_r.at[k, 1])
        part[four(2), right] = (
            part[four(2), right].astype(F32) + a_m[:, slot].astype(F32)
        ).astype(BF16)
        send(part.at[four(2), chunk], b_m.at[:, chunk], b_s.at[k, 1], b_r.at[k, 1], to_zd)

    def close(k):
        chunk = pl.ds(k * CH, CH)
        arrived(b_p.at[:, chunk], b_r.at[k, 0])
        arrived(b_m.at[:, chunk], b_r.at[k, 1])
        total = (
            residual[:, chunk].astype(F32) + part[four(3), chunk].astype(F32)
            + b_p[:, chunk].astype(F32) + b_m[:, chunk].astype(F32)
        )
        upd[:, chunk] = total
        return jnp.sum(total * total, axis=-1, keepdims=True)

    arrived(nrecv.at[four(0)], n_r.at[0])
    far(0)
    mirror(0, 2)
    far(1)
    relay(0, 5)
    for j in range(1, 4):
        arrived(nrecv.at[four(j)], n_r.at[j])
    mirror(0, 3)
    far(2)
    join(0)
    mirror(0, 4)
    far(3)
    relay(0, 6)
    join(1)
    mirror(0, 5)
    far(4)
    join(2)
    relay(0, 7)
    mirror(0, 6)
    far(5)
    join(3)
    mirror(0, 7)
    far(6)
    join(4)
    far(7)
    join(5)
    join(6)
    join(7)
    kvbuf[:, :, :, pl.ds(256, HEAD)] = jnp.ones((24, NP, R, HEAD), BF16)
    own[2].wait()
    separate(wkv_own, wq_own, 0, MODEL)
    relay(1, 0)
    relay(2, 0)
    square = close(0)
    for k in range(1, 4):
        square += close(k)
    relay(1, 1)
    relay(2, 1)
    square += close(4)
    square += close(5)
    mirror(1, 0)
    mirror(2, 0)
    square += close(6)
    square += close(7)
    scale = lax.rsqrt(square * (1.0 / MODEL) + EPS)
    store = pltpu.make_async_copy(upd, upd_out, own_sem.at[3])
    store.start()

    for p in range(NP):
        row = pl.ds(p * R, R)
        gath[p, z] = (upd[row, :] * scale[p * R : (p + 1) * R] * again[...]).astype(BF16)
        mine = gath.at[p, z]
        send(mine, mine, g_s.at[p, 0], g_r.at[p, 0], to_zu)
        send(mine, mine, g_s.at[p, 1], g_r.at[p, 1], to_zd)

    def forward(p):
        below, above = gath.at[p, z_dn], gath.at[p, z_up]
        left, right = pl.ds(0, MODEL // 2), pl.ds(MODEL // 2, MODEL // 2)
        arrived(below, g_r.at[p, 0])
        send(below.at[:, left], below.at[:, left], g_s.at[p, 2], g_r.at[p, 2], to_zu)
        arrived(above, g_r.at[p, 1])
        send(above.at[:, right], above.at[:, right], g_s.at[p, 3], g_r.at[p, 3], to_zd)

    def gathered(p):
        far = gath.at[p, z_far]
        arrived(far.at[:, pl.ds(0, MODEL // 2)], g_r.at[p, 2])
        arrived(far.at[:, pl.ds(MODEL // 2, MODEL // 2)], g_r.at[p, 3])

    kv = pl.ds(0, 256)
    mine_half, mine_kv = pl.ds(xl * 4, 4), pl.ds(16 + xl * 4, 4)

    def second(p):
        acc[...] = jnp.zeros_like(acc)

        def deep(j, carry):
            at = pl.ds(pl.multiple_of(j * 1024, 1024), 1024)
            lhs = gath[p, :, :, at].reshape(4 * R, 1024)
            acc[:, pl.ds(0, QKV)] += dot(lhs, wq_own[at, :])
            acc[:, pl.ds(QKV, QKV)] += dot(lhs, wq_par[at, :])
            return carry

        lax.fori_loop(0, 6, deep, 0)
        stkv[p] = acc[:, pl.ds(QKV + 512, 256)].astype(BF16).reshape(4, R, 256)
        kvbuf[mine_kv, p, :, kv] = acc[:, pl.ds(512, 256)].astype(BF16).reshape(4, R, 256)
        send(stkv.at[p], kvbuf.at[mine_kv, p, :, kv], x_s.at[p, 0], x_r.at[p, 0], to_pair)
        for step in (1, 2):

            @pl.when(s + step < 16)
            def _(step=step):
                slot = kvbuf.at[pl.ds(16 - 8 * step + xl * 4, 4), p, :, kv]
                sem = h_r.at[p, step - 1, xl]
                send(kvbuf.at[mine_kv, p, :, kv], slot, h_s.at[p, step - 1, 0], sem, (s + step, h), False)
                send(stkv.at[p], slot, h_s.at[p, step - 1, 1], sem, (s + step, other), False)

        stq[p] = acc[:, pl.ds(QKV, 512)].astype(BF16).reshape(4, R, 512)
        send(stq.at[p], qbuf.at[mine_half, p], x_s.at[p, 1], x_r.at[p, 1], to_pair)
        qbuf[mine_half, p] = acc[:, pl.ds(0, 512)].astype(BF16).reshape(4, R, 512)

    for k in (2, 3):
        relay(1, k)
        relay(2, k)
        mirror(1, k - 1)
        mirror(2, k - 1)
    forward(0)
    mirror(1, 3)
    mirror(2, 3)
    forward(1)
    for k in range(4):
        separate(wkv_par, wq_par, c * 3072 + k * 768, 768)
    own[1].wait()
    for k in range(4):
        ready(1, k)
        ready(2, k)
        separate(wkv_par, wq_par, (1 - c) * 3072 + k * 768, 768)
    gathered(0)
    second(0)
    gathered(1)
    second(1)

    @pl.when(s < 1)
    def _():
        kvbuf[pl.ds(8, 8), :, :, kv] = jnp.zeros((8, NP, R, 256), BF16)

    @pl.when(s < 2)
    def _():
        kvbuf[pl.ds(0, 8), :, :, kv] = jnp.zeros((8, NP, R, 256), BF16)

    for p in range(NP):
        arrived(kvbuf.at[pl.ds(16 + (1 - xl) * 4, 4), p, :, kv], x_r.at[p, 0])
        for step in (1, 2):

            @pl.when(s - step >= 0)
            def _(p=p, step=step):
                for hf in (0, 1):
                    slot = kvbuf.at[pl.ds(16 - 8 * step + hf * 4, 4), p, :, kv]
                    arrived(slot, h_r.at[p, step - 1, hf])

        arrived(qbuf.at[pl.ds((1 - xl) * 4, 4), p], x_r.at[p, 1])

    factor = HEAD**-0.5 * 1.4426950408889634

    def attend(t, carry):
        row, col = rows_of((HEAD, 1)), cols_of((HEAD, 640))
        early = 1024 - s * TOK - t * HEAD
        middle = cols_of((HEAD, 384)) + 640 >= early
        last = cols_of((HEAD, HEAD)) <= row
        keys = kvbuf[pl.ds(2 * t, 18), :, :, pl.ds(0, HEAD)].reshape(1152, HEAD)
        vals = kvbuf[pl.ds(2 * t, 18), :, :, pl.ds(HEAD, 256)].reshape(1152, 256)
        for i in range(4):
            first = jnp.maximum(row + (1025 - window[h * 4 + i]), early)
            q = qbuf[pl.ds(2 * t, 2), :, :, head_of(i)].reshape(HEAD, HEAD)
            sc = dot_t(q, keys)
            sc = jnp.concatenate(
                (
                    jnp.where(col >= first, sc[:, :640], -1e30),
                    jnp.where(middle, sc[:, 640:1024], -1e30),
                    jnp.where(last, sc[:, 1024:], -1e30),
                ),
                axis=1,
            )
            top = jnp.max(sc, axis=-1, keepdims=True)
            pr = jnp.exp2((sc - top) * factor).astype(BF16)
            both = dot(pr, vals)
            out = both[:, :HEAD] / both[:, HEAD:]
            att_out[pl.ds(pl.multiple_of(t * HEAD, HEAD), HEAD), head_of(i)] = out.astype(BF16)
        return carry

    lax.fori_loop(0, 4, attend, 0)

    store.wait()
    for cp in sent:
        cp.wait_send()
    for mm in range(1, 8):

        @pl.when(m < mm)
        def _(mm=mm):
            pltpu.make_async_copy(t_send, t_send, t_s.at[mm - 1]).wait()

    for p in range(NP):
        for step in (1, 2):

            @pl.when(s + step < 16)
            def _(p=p, step=step):
                pltpu.make_async_copy(stkv.at[p], stkv.at[p], h_s.at[p, step - 1, 0]).wait()
                pltpu.make_async_copy(stkv.at[p], stkv.at[p], h_s.at[p, step - 1, 1]).wait()


def on_device(
    lightning_qkv,
    residual,
    decay_rate,
    lightning_gain,
    out_weight,
    attn_gain,
    query_weight,
    key_value_weight,
    window,
):
    vmem = pl.BlockSpec(memory_space=pltpu.VMEM)
    smem = pl.BlockSpec(memory_space=pltpu.SMEM)
    anyw = pl.BlockSpec(memory_space=pl.ANY)
    dma = pltpu.SemaphoreType.DMA
    V = pltpu.VMEM
    return pl.pallas_call(
        body,
        out_shape=(
            jax.ShapeDtypeStruct((64, MODEL), F32),
            jax.ShapeDtypeStruct((TOK, 512), BF16),
        ),
        in_specs=[vmem, vmem, smem, vmem, anyw, vmem, anyw, anyw, smem],
        out_specs=(anyw, vmem),
        scratch_shapes=[
            V((512, MODEL), BF16),
            V((512, MODEL), BF16),
            V((MODEL, QKV), BF16),
            V((MODEL, QKV), BF16),
            V((2 * MODEL, HEAD), BF16),
            V((2 * MODEL, HEAD), BF16),
            V((768, HEAD), F32),
            V((4, HEAD, HEAD), F32),
            V((4, HEAD, HEAD), F32),
            V((2, HEAD, HEAD), BF16),
            V((7, 2, HEAD, HEAD), BF16),
            V((4, HEAD, HEAD), F32),
            V((TOK, 512), F32),
            V((256, 512), BF16),
            V((256, 512), BF16),
            V((256, 512), BF16),
            V((256, MODEL), BF16),
            V((64, MODEL // 2), BF16),
            V((64, MODEL // 2), BF16),
            V((64, MODEL), BF16),
            V((64, MODEL), BF16),
            V((64, MODEL), F32),
            V((NP, 4, R, MODEL), BF16),
            V((4 * R, 2 * QKV), F32),
            V((8, NP, R, 512), BF16),
            V((24, NP, R, 384), BF16),
            V((NP, 4, R, 512), BF16),
            V((NP, 4, R, 256), BF16),
            dma((4,)),
            dma((3, NCH, 5)),
            dma((3, NCH, 5)),
            dma((2,)),
            dma((2,)),
            dma((7,)),
            dma((7,)),
            dma((4,)),
            dma((4,)),
            dma((NCH, 2)),
            dma((NCH, 2)),
            dma((NCH, 2)),
            dma((NCH, 2)),
            dma((NP, 4)),
            dma((NP, 4)),
            dma((NP, 2)),
            dma((NP, 2)),
            dma((NP, 2, 2)),
            dma((NP, 2, 2)),
        ],
        compiler_params=pltpu.CompilerParams(
            collective_id=0, has_side_effects=True, vmem_limit_bytes=60 * 2**20
        ),
    )(
        jnp.transpose(lightning_qkv, (1, 0, 2)),
        residual,
        decay_rate,
        lightning_gain.reshape(1, 512),
        out_weight,
        attn_gain.reshape(1, MODEL),
        query_weight,
        key_value_weight.reshape(2 * MODEL, HEAD),
        window,
    )


def solution(mesh):
    placed = (
        P("seq", None, "head"),
        P(("seq", "head"), None),
        P(),
        P("head"),
        P("head", None),
        P(),
        P(None, "head"),
        P(None, "head", None, None),
        P(),
    )
    return jax.shard_map(
        on_device,
        mesh=mesh,
        in_specs=placed,
        out_specs=(P(("seq", "head"), None), P("seq", "head")),
        check_vma=False,
    )
```

```python
import functools

import jax
import jax.numpy as jnp
from jax import lax
from jax.experimental import pallas as pl
from jax.experimental.pallas import tpu as pltpu
from jax.sharding import PartitionSpec as P

MESH = pl.DeviceIdType.MESH
F32 = jnp.float32
BF16 = jnp.bfloat16
HEAD = 128
EPS = 1e-06
TOK = 512
MODEL = 6144
NCH = 8
CH = MODEL // NCH
HALF = CH // 2
NP = 2
R = 64 // NP
QKV = 768


def coords():
    s, h = lax.axis_index("seq"), lax.axis_index("head")
    return lax.div(s, 8), lax.rem(lax.div(s, 2), 4), lax.rem(s, 2), lax.div(h, 4), lax.rem(h, 4)


def place(x, y, c, z):
    x, y, z = lax.rem(x + 4, 4), lax.rem(y + 4, 4), lax.rem(z + 4, 4)
    return (lax.div(x, 2) * 8 + y * 2 + c, lax.rem(x, 2) * 4 + z)


def dot(a, b):
    return jnp.dot(a, b, preferred_element_type=F32)


def dot_t(a, b):
    return lax.dot_general(a, b, (((1,), (1,)), ((), ())), preferred_element_type=F32)


def rows_of(shape):
    return lax.broadcasted_iota(jnp.int32, shape, 0)


def cols_of(shape):
    return lax.broadcasted_iota(jnp.int32, shape, 1)


def body(
    qkv,
    residual,
    decay,
    lgain,
    wo_hbm,
    again,
    wq_hbm,
    wkv_hbm,
    window,
    upd_out,
    att_out,
    wo_own,
    wo_par,
    wq_own,
    wq_par,
    wkv_own,
    wkv_par,
    wide,
    s_own,
    s_pair,
    t_send,
    t_recv,
    p_all,
    intra,
    nsend,
    nown,
    nrecv,
    part,
    a_p,
    a_m,
    b_p,
    b_m,
    upd,
    gath,
    scales,
    acc,
    qbuf,
    kvbuf,
    stq,
    stkv,
    own_sem,
    w_s,
    w_r,
    sp_s,
    sp_r,
    t_s,
    t_r,
    n_s,
    n_r,
    a_s,
    a_r,
    b_s,
    b_r,
    g_s,
    g_r,
    l_s,
    l_r,
    x_s,
    x_r,
    h_s,
    h_r,
):
    xh, y, c, xl, z = coords()
    x = 2 * xh + xl
    s, h = lax.axis_index("seq"), lax.axis_index("head")
    other = lax.rem(h + 4, 8)
    m = xh * 4 + y
    e = lax.rem(y, 2)
    z_up, z_dn = lax.rem(z + 1, 4), lax.rem(z + 3, 4)
    z_far = lax.rem(z + 2, 4)
    to_zu, to_zd = place(x, y, c, z + 1), place(x, y, c, z - 1)
    to_outer = place(x + 2 * xl - 1, y, c, z)
    to_yu, to_yd = place(x, y + 1, c, z), place(x, y - 1, c, z)
    to_core = (s + 1 - 2 * c, h)
    to_pair = (s, other)
    sent = []

    def send(src, dst, ssem, rsem, target, later=True):
        cp = pltpu.make_async_remote_copy(
            src_ref=src, dst_ref=dst, send_sem=ssem, recv_sem=rsem,
            device_id=target, device_id_type=MESH,
        )
        cp.start()
        if later:
            sent.append(cp)
        return cp

    def arrived(dst, sem):
        pltpu.make_async_copy(dst, dst, sem).wait()

    bar = pltpu.get_barrier_semaphore()
    peers = [to_zu, to_zd, to_pair, to_outer, to_core]
    for k in range(1, 8):
        mm = lax.rem(m + k, 8)
        peers.append((mm * 2 + c, h))
    for step in (1, 2, 14, 15):
        there = lax.rem(s + step, 16)
        peers += [(there, h), (there, other)]
    for p in peers:
        pl.semaphore_signal(bar, 1, device_id=p, device_id_type=MESH)

    own = [
        pltpu.make_async_copy(wo_hbm, wo_own, own_sem.at[0]),
        pltpu.make_async_copy(wq_hbm, wq_own.at[:, pl.ds(0, 512)], own_sem.at[1]),
        pltpu.make_async_copy(wkv_hbm, wkv_own, own_sem.at[2]),
    ]

    hbm_of = (wo_hbm, wq_hbm, wkv_hbm)

    def region(a, k, cc, par, d, hbm=False):
        whole, cut = (128, 48) if a == 0 else (384 * a, 176 * a)
        base = cc * 256 if a == 0 else cc * 8 * whole + k * 2 * whole
        count = (cut, whole - cut, 2 * whole)[d]
        base = base + par * whole + (cut if d == 1 else 0)
        rows = pl.ds(pl.multiple_of(base, 16), count)
        if a == 0:
            return (wo_hbm if hbm else wo_par).at[rows, pl.ds(k * CH, CH)]
        if hbm:
            return hbm_of[a].at[rows]
        return wq_par.at[rows, pl.ds(0, 512)] if a == 1 else wkv_par.at[rows]

    def push(a, k, d):
        send(
            region(a, k, c, e, d, True), region(a, k, c, e, d),
            w_s.at[a, k, d], w_r.at[a, k, d], (to_pair, to_outer)[d],
        )

    def relay(a, k):
        for d in (0, 1):
            piece = region(a, k, c, e, d)
            arrived(piece, w_r.at[a, k, d])
            target = (to_yu, to_yd)[(d + k) % 2]
            send(piece, piece, w_s.at[a, k, 2 + d], w_r.at[a, k, 2 + d], target)

    def mirror(a, k):
        for d in (0, 1):
            arrived(region(a, k, c, 1 - e, d), w_r.at[a, k, 2 + d])
        piece = region(a, k, c, 0, 2)
        send(piece, piece, w_s.at[a, k, 4], w_r.at[a, k, 4], to_core)

    def ready(a, k):
        arrived(region(a, k, 1 - c, 0, 2), w_r.at[a, k, 4])

    def separate(raw, to, first, count):
        def piece(j, carry):
            at = pl.multiple_of(first + j * 384, 64)
            wide[...] = raw[pl.ds(pl.multiple_of(2 * at, 128), 768), :].astype(F32)
            for i in (0, 1):
                cols = pl.ds(512 + i * HEAD, HEAD)
                to[pl.ds(at, 384), cols] = wide[pl.ds(i, 384, stride=2), :].astype(BF16)
            return carry

        lax.fori_loop(0, count // 384, piece, 0)

    for cp in own:
        cp.start()

    rate = [decay[h * 4 + i] for i in range(4)]

    def head_of(i):
        return pl.ds(i * HEAD, HEAD)

    for i in range(4):
        back = (TOK - 1 - rows_of((TOK, HEAD))).astype(F32)
        keys = qkv[1, :, head_of(i)].astype(F32) * jnp.exp(-rate[i] * back)
        s_own[i] = lax.dot_general(
            keys.astype(BF16), qkv[2, :, head_of(i)], (((0,), (0,)), ((), ())),
            preferred_element_type=F32,
        )
    pl.semaphore_wait(bar, len(peers))
    push(0, 0, 1)
    push(0, 0, 0)
    send(s_own, s_pair, sp_s.at[0], sp_r.at[0], to_core)

    def within(i):
        for t in range(4):
            n = HEAD * (t + 1)
            lq = qkv[0, pl.ds(t * HEAD, HEAD), head_of(i)]
            sc = dot_t(lq, qkv[1, pl.ds(0, n), head_of(i)])
            gap = (rows_of((HEAD, n)) + t * HEAD - cols_of((HEAD, n))).astype(F32)
            fade = jnp.where(gap >= 0, jnp.exp(-rate[i] * jnp.maximum(gap, 0.0)), 0.0)
            intra[pl.ds(t * HEAD, HEAD), head_of(i)] = dot(
                (sc * fade).astype(BF16), qkv[2, pl.ds(0, n), head_of(i)]
            )

    within(0)
    arrived(s_pair, sp_r.at[0])
    for i in range(2):
        hd = 2 * c + i
        dd = decay[h * 4 + hd]
        mine, theirs = s_own[hd], s_pair[hd]
        fade = jnp.exp(jnp.full((HEAD, HEAD), -dd * TOK, F32))
        first, second = jnp.where(c == 0, mine, theirs), jnp.where(c == 0, theirs, mine)
        t_send[i] = (fade * first + second).astype(BF16)
    for mm in range(1, 8):

        @pl.when(m < mm)
        def _(mm=mm):
            send(t_send, t_recv.at[m], t_s.at[mm - 1], t_r.at[m], (mm * 2 + c, h), False)

    for k in range(1, NCH):
        push(0, k, 1)
    for k in range(1, 6):
        push(0, k, 0)
    for k in range(4):
        push(1, k, 1)
        push(2, k, 1)
    within(1)
    within(2)
    within(3)
    relay(0, 0)
    relay(0, 1)
    for i in range(2):
        p_all[2 * c + i] = jnp.zeros((HEAD, HEAD), F32)
    for mm in range(7):

        @pl.when(mm < m)
        def _(mm=mm):
            arrived(t_recv.at[mm], t_r.at[mm])
            for i in range(2):
                dd = decay[h * 4 + 2 * c + i]
                gone = (m - 1 - mm).astype(F32) * (2.0 * TOK)
                p_all[2 * c + i] += (
                    jnp.exp(jnp.full((HEAD, HEAD), -dd * gone, F32)) * t_recv[mm, i].astype(F32)
                )

    half_p = p_all.at[pl.ds(2 * c, 2)]
    across = send(half_p, half_p, sp_s.at[1], sp_r.at[1], to_core, False)
    relay(0, 2)
    arrived(p_all.at[pl.ds(2 * (1 - c), 2)], sp_r.at[1])

    order = (z_far, z_up, z_dn, z)

    def finish(to, lo, j):
        first = lo + order[j] * 64
        span, out = pl.ds(pl.multiple_of(first, 64), 64), pl.ds(j * 64, 64)
        for i in range(4):
            ahead = (rows_of((64, HEAD)) + (first + 1)).astype(F32)
            lq = qkv[0, span, head_of(i)].astype(F32) * jnp.exp(-rate[i] * ahead)
            full = intra[span, head_of(i)] + jnp.dot(
                lq, p_all[i], preferred_element_type=F32, precision=lax.Precision.HIGHEST
            )
            scale = lax.rsqrt(jnp.mean(full * full, axis=-1, keepdims=True) + EPS)
            to[out, head_of(i)] = (full * scale * lgain[:, head_of(i)]).astype(BF16)

    def four(j):
        return pl.ds(j * 64, 64)

    across.wait_send()

    @pl.when(c == 1)
    def _():
        for i in range(4):
            fade = jnp.exp(jnp.full((HEAD, HEAD), -rate[i] * TOK, F32))
            p_all[i] = fade * p_all[i] + s_pair[i]

    for j in range(4):
        finish(nsend, (1 - xl) * 256, j)
        send(nsend.at[four(j)], nrecv.at[four(j)], n_s.at[j], n_r.at[j], to_pair)
    push(0, 6, 0)
    push(0, 7, 0)
    for k in range(4):
        push(1, k, 0)
        push(2, k, 0)
    relay(0, 3)
    mirror(0, 0)
    for j in range(4):
        finish(nown, xl * 256, j)
    mirror(0, 1)
    relay(0, 4)
    own[0].wait()

    def project(k, lo, count):
        at, rows = pl.ds(k * CH, CH), pl.ds(lo, count)
        total = dot(nown[rows, :], wo_own[:, at]) + dot(nrecv[rows, :], wo_par[:, at])
        part[k, rows] = total.astype(BF16)

    low, high = pl.ds(0, 32), pl.ds(32, 32)

    def far(k):
        ready(0, k)
        project(k, 0, 64)
        send(part.at[k, low], a_p.at[k], a_s.at[k, 0], a_r.at[k, 0], to_zu)
        send(part.at[k, high], a_m.at[k], a_s.at[k, 1], a_r.at[k, 1], to_zd)

    def join(k):
        project(k, 64, 192)
        one, two = pl.ds(64, 32), pl.ds(160, 32)
        arrived(a_p.at[k], a_r.at[k, 0])
        part[k, one] = (part[k, one].astype(F32) + a_p[k].astype(F32)).astype(BF16)
        send(part.at[k, four(1)], b_p.at[k], b_s.at[k, 0], b_r.at[k, 0], to_zu)
        arrived(a_m.at[k], a_r.at[k, 1])
        part[k, two] = (part[k, two].astype(F32) + a_m[k].astype(F32)).astype(BF16)
        send(part.at[k, four(2)], b_m.at[k], b_s.at[k, 1], b_r.at[k, 1], to_zd)

    def close(k):
        chunk = pl.ds(k * CH, CH)
        arrived(b_p.at[k], b_r.at[k, 0])
        arrived(b_m.at[k], b_r.at[k, 1])
        total = (
            residual[:, chunk].astype(F32) + part[k, four(3)].astype(F32)
            + b_p[k].astype(F32) + b_m[k].astype(F32)
        )
        upd[:, chunk] = total
        return jnp.sum(total * total, axis=-1, keepdims=True)

    arrived(nrecv.at[four(0)], n_r.at[0])
    far(0)
    mirror(0, 2)
    far(1)
    relay(0, 5)
    for j in range(1, 4):
        arrived(nrecv.at[four(j)], n_r.at[j])
    mirror(0, 3)
    far(2)
    join(0)
    mirror(0, 4)
    far(3)
    relay(0, 6)
    join(1)
    mirror(0, 5)
    far(4)
    join(2)
    relay(0, 7)
    mirror(0, 6)
    far(5)
    join(3)
    mirror(0, 7)
    far(6)
    join(4)
    far(7)
    join(5)
    join(6)
    join(7)
    kvbuf[:, :, :, pl.ds(256, HEAD)] = jnp.ones((24, NP, R, HEAD), BF16)
    own[2].wait()
    separate(wkv_own, wq_own, 0, MODEL)
    square = close(0)
    for k in range(1, 4):
        square += close(k)

    first_rows, wide_half = pl.ds(0, R), MODEL // 2

    def early(i):
        cols = pl.ds(i * wide_half, wide_half)
        gath[0, z, :, cols] = (upd[first_rows, cols] * again[:, cols]).astype(BF16)
        mine = gath.at[0, z, :, cols]
        send(mine, mine, g_s.at[0, 2 * i], g_r.at[0, 2 * i], to_zu)
        send(mine, mine, g_s.at[0, 2 * i + 1], g_r.at[0, 2 * i + 1], to_zd)

    early(0)
    relay(1, 0)
    relay(2, 0)
    square += close(4)
    square += close(5)
    square += close(6)
    square += close(7)
    early(1)
    scale = lax.rsqrt(square * (1.0 / MODEL) + EPS)
    scales[z] = jnp.broadcast_to(scale[:R], (R, HEAD))
    for i, target in enumerate((to_zu, to_zd, place(x, y, c, z + 2))):
        send(scales.at[z], scales.at[z], l_s.at[i], l_r.at[i], target)
    row = pl.ds(R, R)
    gath[1, z] = (upd[row, :] * scale[R:] * again[...]).astype(BF16)
    mine = gath.at[1, z]
    send(mine, mine, g_s.at[1, 0], g_r.at[1, 0], to_zu)
    send(mine, mine, g_s.at[1, 1], g_r.at[1, 1], to_zd)
    store = pltpu.make_async_copy(upd, upd_out, own_sem.at[3])
    store.start()
    relay(1, 1)
    relay(2, 1)
    mirror(1, 0)
    mirror(2, 0)

    up_rows, dn_rows = pl.ds(0, R // 2), pl.ds(R // 2, R // 2)

    def forward(p):
        below, above = gath.at[p, z_dn], gath.at[p, z_up]
        for d, block in ((0, below), (1, above)):
            if p == 0:
                for i in (0, 1):
                    arrived(block.at[:, pl.ds(i * wide_half, wide_half)], g_r.at[0, 2 * i + d])
            else:
                arrived(block, g_r.at[p, d])
            half = block.at[(up_rows, dn_rows)[d]]
            send(half, half, g_s.at[p, 4 + d], g_r.at[p, 4 + d], (to_zu, to_zd)[d])

    def gathered(p):
        arrived(gath.at[p, z_far, up_rows], g_r.at[p, 4])
        arrived(gath.at[p, z_far, dn_rows], g_r.at[p, 5])
        if p == 0:
            for i, there in enumerate((z_dn, z_up, z_far)):
                arrived(scales.at[there], l_r.at[i])

    kv = pl.ds(0, 256)
    mine_half, mine_kv = pl.ds(xl * 4, 4), pl.ds(16 + xl * 4, 4)

    def second(p):
        def product(weight, first, count, to):
            out = pl.ds(to, count)
            acc[:, out] = jnp.zeros((4 * R, count), F32)

            def deep(j, carry):
                at = pl.ds(pl.multiple_of(j * 1024, 1024), 1024)
                lhs = gath[p, :, :, at].reshape(4 * R, 1024)
                acc[:, out] += dot(lhs, weight[at, pl.ds(first, count)])
                return carry

            lax.fori_loop(0, 6, deep, 0)
            if p == 0:
                acc[:, out] *= scales[...].reshape(4 * R, HEAD)[:, :1]

        product(wq_par, 512, 256, QKV + 512)
        product(wq_own, 512, 256, 512)
        stkv[p] = acc[:, pl.ds(QKV + 512, 256)].astype(BF16).reshape(4, R, 256)
        kvbuf[mine_kv, p, :, kv] = acc[:, pl.ds(512, 256)].astype(BF16).reshape(4, R, 256)
        send(stkv.at[p], kvbuf.at[mine_kv, p, :, kv], x_s.at[p, 0], x_r.at[p, 0], to_pair)
        for step in (1, 2):

            @pl.when(s + step < 16)
            def _(step=step):
                slot = kvbuf.at[pl.ds(16 - 8 * step + xl * 4, 4), p, :, kv]
                sem = h_r.at[p, step - 1, xl]
                send(kvbuf.at[mine_kv, p, :, kv], slot, h_s.at[p, step - 1, 0], sem, (s + step, h), False)
                send(stkv.at[p], slot, h_s.at[p, step - 1, 1], sem, (s + step, other), False)

        product(wq_par, 0, 512, QKV)
        stq[p] = acc[:, pl.ds(QKV, 512)].astype(BF16).reshape(4, R, 512)
        send(stq.at[p], qbuf.at[mine_half, p], x_s.at[p, 1], x_r.at[p, 1], to_pair)
        product(wq_own, 0, 512, 0)
        qbuf[mine_half, p] = acc[:, pl.ds(0, 512)].astype(BF16).reshape(4, R, 512)

    for k in (2, 3):
        relay(1, k)
        relay(2, k)
        mirror(1, k - 1)
        mirror(2, k - 1)
    forward(0)
    mirror(1, 3)
    mirror(2, 3)
    forward(1)
    for k in range(4):
        separate(wkv_par, wq_par, c * 3072 + k * 768, 768)
    own[1].wait()
    for k in range(4):
        ready(1, k)
        ready(2, k)
        separate(wkv_par, wq_par, (1 - c) * 3072 + k * 768, 768)
    gathered(0)
    second(0)
    gathered(1)
    second(1)

    @pl.when(s < 1)
    def _():
        kvbuf[pl.ds(8, 8), :, :, kv] = jnp.zeros((8, NP, R, 256), BF16)

    @pl.when(s < 2)
    def _():
        kvbuf[pl.ds(0, 8), :, :, kv] = jnp.zeros((8, NP, R, 256), BF16)

    for p in range(NP):
        arrived(kvbuf.at[pl.ds(16 + (1 - xl) * 4, 4), p, :, kv], x_r.at[p, 0])
        for step in (1, 2):

            @pl.when(s - step >= 0)
            def _(p=p, step=step):
                for hf in (0, 1):
                    slot = kvbuf.at[pl.ds(16 - 8 * step + hf * 4, 4), p, :, kv]
                    arrived(slot, h_r.at[p, step - 1, hf])

        arrived(qbuf.at[pl.ds((1 - xl) * 4, 4), p], x_r.at[p, 1])

    factor = HEAD**-0.5 * 1.4426950408889634

    def attend(t, carry):
        row, col = rows_of((HEAD, 1)), cols_of((HEAD, 640))
        early = 1024 - s * TOK - t * HEAD
        middle = cols_of((HEAD, 384)) + 640 >= early
        last = cols_of((HEAD, HEAD)) <= row
        keys = kvbuf[pl.ds(2 * t, 18), :, :, pl.ds(0, HEAD)].reshape(1152, HEAD)
        vals = kvbuf[pl.ds(2 * t, 18), :, :, pl.ds(HEAD, 256)].reshape(1152, 256)
        for i in range(4):
            first = jnp.maximum(row + (1025 - window[h * 4 + i]), early)
            q = qbuf[pl.ds(2 * t, 2), :, :, head_of(i)].reshape(HEAD, HEAD)
            sc = dot_t(q, keys)
            sc = jnp.concatenate(
                (
                    jnp.where(col >= first, sc[:, :640], -1e30),
                    jnp.where(middle, sc[:, 640:1024], -1e30),
                    jnp.where(last, sc[:, 1024:], -1e30),
                ),
                axis=1,
            )
            top = jnp.max(sc, axis=-1, keepdims=True)
            pr = jnp.exp2((sc - top) * factor).astype(BF16)
            both = dot(pr, vals)
            out = both[:, :HEAD] / both[:, HEAD:]
            att_out[pl.ds(pl.multiple_of(t * HEAD, HEAD), HEAD), head_of(i)] = out.astype(BF16)
        return carry

    lax.fori_loop(0, 4, attend, 0)

    store.wait()
    for cp in sent:
        cp.wait_send()
    for mm in range(1, 8):

        @pl.when(m < mm)
        def _(mm=mm):
            pltpu.make_async_copy(t_send, t_send, t_s.at[mm - 1]).wait()

    for p in range(NP):
        for step in (1, 2):

            @pl.when(s + step < 16)
            def _(p=p, step=step):
                pltpu.make_async_copy(stkv.at[p], stkv.at[p], h_s.at[p, step - 1, 0]).wait()
                pltpu.make_async_copy(stkv.at[p], stkv.at[p], h_s.at[p, step - 1, 1]).wait()


def on_device(
    lightning_qkv,
    residual,
    decay_rate,
    lightning_gain,
    out_weight,
    attn_gain,
    query_weight,
    key_value_weight,
    window,
):
    vmem = pl.BlockSpec(memory_space=pltpu.VMEM)
    smem = pl.BlockSpec(memory_space=pltpu.SMEM)
    anyw = pl.BlockSpec(memory_space=pl.ANY)
    dma = pltpu.SemaphoreType.DMA
    V = pltpu.VMEM
    return pl.pallas_call(
        body,
        out_shape=(
            jax.ShapeDtypeStruct((64, MODEL), F32),
            jax.ShapeDtypeStruct((TOK, 512), BF16),
        ),
        in_specs=[vmem, vmem, smem, vmem, anyw, vmem, anyw, anyw, smem],
        out_specs=(anyw, vmem),
        scratch_shapes=[
            V((512, MODEL), BF16),
            V((512, MODEL), BF16),
            V((MODEL, QKV), BF16),
            V((MODEL, QKV), BF16),
            V((2 * MODEL, HEAD), BF16),
            V((2 * MODEL, HEAD), BF16),
            V((768, HEAD), F32),
            V((4, HEAD, HEAD), F32),
            V((4, HEAD, HEAD), F32),
            V((2, HEAD, HEAD), BF16),
            V((7, 2, HEAD, HEAD), BF16),
            V((4, HEAD, HEAD), F32),
            V((TOK, 512), F32),
            V((256, 512), BF16),
            V((256, 512), BF16),
            V((256, 512), BF16),
            V((NCH, 256, CH), BF16),
            V((NCH, 32, CH), BF16),
            V((NCH, 32, CH), BF16),
            V((NCH, 64, CH), BF16),
            V((NCH, 64, CH), BF16),
            V((64, MODEL), F32),
            V((NP, 4, R, MODEL), BF16),
            V((4, R, HEAD), F32),
            V((4 * R, 2 * QKV), F32),
            V((8, NP, R, 512), BF16),
            V((24, NP, R, 384), BF16),
            V((NP, 4, R, 512), BF16),
            V((NP, 4, R, 256), BF16),
            dma((4,)),
            dma((3, NCH, 5)),
            dma((3, NCH, 5)),
            dma((2,)),
            dma((2,)),
            dma((7,)),
            dma((7,)),
            dma((4,)),
            dma((4,)),
            dma((NCH, 2)),
            dma((NCH, 2)),
            dma((NCH, 2)),
            dma((NCH, 2)),
            dma((NP, 6)),
            dma((NP, 6)),
            dma((3,)),
            dma((3,)),
            dma((NP, 2)),
            dma((NP, 2)),
            dma((NP, 2, 2)),
            dma((NP, 2, 2)),
        ],
        compiler_params=pltpu.CompilerParams(
            collective_id=0, has_side_effects=True, vmem_limit_bytes=60 * 2**20
        ),
    )(
        jnp.transpose(lightning_qkv, (1, 0, 2)),
        residual,
        decay_rate,
        lightning_gain.reshape(1, 512),
        out_weight,
        attn_gain.reshape(1, MODEL),
        query_weight,
        key_value_weight.reshape(2 * MODEL, HEAD),
        window,
    )


def solution(mesh):
    placed = (
        P("seq", None, "head"),
        P(("seq", "head"), None),
        P(),
        P("head"),
        P("head", None),
        P(),
        P(None, "head"),
        P(None, "head", None, None),
        P(),
    )
    return jax.shard_map(
        on_device,
        mesh=mesh,
        in_specs=placed,
        out_specs=(P(("seq", "head"), None), P("seq", "head")),
        check_vma=False,
    )
```

```python
import functools

import jax
import jax.numpy as jnp
from jax import lax
from jax.experimental import pallas as pl
from jax.experimental.pallas import tpu as pltpu
from jax.sharding import PartitionSpec as P

MESH = pl.DeviceIdType.MESH
F32 = jnp.float32
BF16 = jnp.bfloat16
HEAD = 128
EPS = 1e-06
TOK = 512
MODEL = 6144
NCH = 8
CH = MODEL // NCH
HALF = CH // 2
NP = 2
R = 64 // NP
QKV = 768


def coords():
    s, h = lax.axis_index("seq"), lax.axis_index("head")
    return lax.div(s, 8), lax.rem(lax.div(s, 2), 4), lax.rem(s, 2), lax.div(h, 4), lax.rem(h, 4)


def place(x, y, c, z):
    x, y, z = lax.rem(x + 4, 4), lax.rem(y + 4, 4), lax.rem(z + 4, 4)
    return (lax.div(x, 2) * 8 + y * 2 + c, lax.rem(x, 2) * 4 + z)


def dot(a, b):
    return jnp.dot(a, b, preferred_element_type=F32)


def dot_t(a, b):
    return lax.dot_general(a, b, (((1,), (1,)), ((), ())), preferred_element_type=F32)


def rows_of(shape):
    return lax.broadcasted_iota(jnp.int32, shape, 0)


def cols_of(shape):
    return lax.broadcasted_iota(jnp.int32, shape, 1)


def body(
    qkv,
    residual,
    decay,
    lgain,
    wo_hbm,
    again,
    wq_hbm,
    wkv_hbm,
    window,
    upd_out,
    att_out,
    wo_own,
    wo_par,
    wq_own,
    wq_par,
    wkv_own,
    wkv_par,
    wide,
    s_own,
    s_pair,
    t_send,
    t_recv,
    p_all,
    intra,
    nsend,
    nown,
    nrecv,
    part,
    a_p,
    a_m,
    b_p,
    b_m,
    upd,
    gath,
    acc,
    qbuf,
    kvbuf,
    stq,
    stkv,
    own_sem,
    w_s,
    w_r,
    sp_s,
    sp_r,
    t_s,
    t_r,
    n_s,
    n_r,
    a_s,
    a_r,
    b_s,
    b_r,
    g_s,
    g_r,
    x_s,
    x_r,
    h_s,
    h_r,
):
    xh, y, c, xl, z = coords()
    x = 2 * xh + xl
    s, h = lax.axis_index("seq"), lax.axis_index("head")
    other = lax.rem(h + 4, 8)
    m = xh * 4 + y
    e = lax.rem(y, 2)
    z_up, z_dn = lax.rem(z + 1, 4), lax.rem(z + 3, 4)
    z_far = lax.rem(z + 2, 4)
    to_zu, to_zd = place(x, y, c, z + 1), place(x, y, c, z - 1)
    to_outer = place(x + 2 * xl - 1, y, c, z)
    to_yu, to_yd = place(x, y + 1, c, z), place(x, y - 1, c, z)
    to_core = (s + 1 - 2 * c, h)
    to_pair = (s, other)
    sent = []

    def send(src, dst, ssem, rsem, target, later=True):
        cp = pltpu.make_async_remote_copy(
            src_ref=src, dst_ref=dst, send_sem=ssem, recv_sem=rsem,
            device_id=target, device_id_type=MESH,
        )
        cp.start()
        if later:
            sent.append(cp)
        return cp

    def arrived(dst, sem):
        pltpu.make_async_copy(dst, dst, sem).wait()

    bar = pltpu.get_barrier_semaphore()
    peers = [to_zu, to_zd, to_pair, to_outer, to_core]
    for k in range(1, 8):
        mm = lax.rem(m + k, 8)
        peers.append((mm * 2 + c, h))
    for step in (1, 2, 14, 15):
        there = lax.rem(s + step, 16)
        peers += [(there, h), (there, other)]
    for p in peers:
        pl.semaphore_signal(bar, 1, device_id=p, device_id_type=MESH)

    own = [
        pltpu.make_async_copy(wo_hbm, wo_own, own_sem.at[0]),
        pltpu.make_async_copy(wq_hbm, wq_own.at[:, pl.ds(0, 512)], own_sem.at[1]),
        pltpu.make_async_copy(wkv_hbm, wkv_own, own_sem.at[2]),
    ]

    hbm_of = (wo_hbm, wq_hbm, wkv_hbm)

    def region(a, k, cc, par, d, hbm=False):
        whole, cut = (128, 48) if a == 0 else (384 * a, 176 * a)
        base = cc * 256 if a == 0 else cc * 8 * whole + k * 2 * whole
        count = (cut, whole - cut, 2 * whole)[d]
        base = base + par * whole + (cut if d == 1 else 0)
        rows = pl.ds(pl.multiple_of(base, 16), count)
        if a == 0:
            return (wo_hbm if hbm else wo_par).at[rows, pl.ds(k * CH, CH)]
        if hbm:
            return hbm_of[a].at[rows]
        return wq_par.at[rows, pl.ds(0, 512)] if a == 1 else wkv_par.at[rows]

    def push(a, k, d):
        send(
            region(a, k, c, e, d, True), region(a, k, c, e, d),
            w_s.at[a, k, d], w_r.at[a, k, d], (to_pair, to_outer)[d],
        )

    def relay(a, k):
        for d in (0, 1):
            piece = region(a, k, c, e, d)
            arrived(piece, w_r.at[a, k, d])
            target = (to_yu, to_yd)[(d + k) % 2]
            send(piece, piece, w_s.at[a, k, 2 + d], w_r.at[a, k, 2 + d], target)

    def mirror(a, k):
        for d in (0, 1):
            arrived(region(a, k, c, 1 - e, d), w_r.at[a, k, 2 + d])
        piece = region(a, k, c, 0, 2)
        send(piece, piece, w_s.at[a, k, 4], w_r.at[a, k, 4], to_core)

    def ready(a, k):
        arrived(region(a, k, 1 - c, 0, 2), w_r.at[a, k, 4])

    def separate(raw, to, first, count):
        def piece(j, carry):
            at = pl.multiple_of(first + j * 384, 64)
            wide[...] = raw[pl.ds(pl.multiple_of(2 * at, 128), 768), :].astype(F32)
            for i in (0, 1):
                cols = pl.ds(512 + i * HEAD, HEAD)
                to[pl.ds(at, 384), cols] = wide[pl.ds(i, 384, stride=2), :].astype(BF16)
            return carry

        lax.fori_loop(0, count // 384, piece, 0)

    for cp in own:
        cp.start()

    rate = [decay[h * 4 + i] for i in range(4)]

    def head_of(i):
        return pl.ds(i * HEAD, HEAD)

    for i in range(4):
        back = (TOK - 1 - rows_of((TOK, HEAD))).astype(F32)
        keys = qkv[1, :, head_of(i)].astype(F32) * jnp.exp(-rate[i] * back)
        s_own[i] = lax.dot_general(
            keys.astype(BF16), qkv[2, :, head_of(i)], (((0,), (0,)), ((), ())),
            preferred_element_type=F32,
        )
    pl.semaphore_wait(bar, len(peers))
    push(0, 0, 1)
    push(0, 0, 0)
    send(s_own, s_pair, sp_s.at[0], sp_r.at[0], to_core)

    def within(i):
        for t in range(4):
            n = HEAD * (t + 1)
            lq = qkv[0, pl.ds(t * HEAD, HEAD), head_of(i)]
            sc = dot_t(lq, qkv[1, pl.ds(0, n), head_of(i)])
            gap = (rows_of((HEAD, n)) + t * HEAD - cols_of((HEAD, n))).astype(F32)
            fade = jnp.where(gap >= 0, jnp.exp(-rate[i] * jnp.maximum(gap, 0.0)), 0.0)
            intra[pl.ds(t * HEAD, HEAD), head_of(i)] = dot(
                (sc * fade).astype(BF16), qkv[2, pl.ds(0, n), head_of(i)]
            )

    within(0)
    arrived(s_pair, sp_r.at[0])
    for i in range(2):
        hd = 2 * c + i
        dd = decay[h * 4 + hd]
        mine, theirs = s_own[hd], s_pair[hd]
        fade = jnp.exp(jnp.full((HEAD, HEAD), -dd * TOK, F32))
        first, second = jnp.where(c == 0, mine, theirs), jnp.where(c == 0, theirs, mine)
        t_send[i] = (fade * first + second).astype(BF16)
    for mm in range(1, 8):

        @pl.when(m < mm)
        def _(mm=mm):
            send(t_send, t_recv.at[m], t_s.at[mm - 1], t_r.at[m], (mm * 2 + c, h), False)

    for k in range(1, NCH):
        push(0, k, 1)
    for k in range(1, 6):
        push(0, k, 0)
    for k in range(4):
        push(1, k, 1)
        push(2, k, 1)
    within(1)
    within(2)
    within(3)
    relay(0, 0)
    relay(0, 1)
    for i in range(2):
        p_all[2 * c + i] = jnp.zeros((HEAD, HEAD), F32)
    for mm in range(7):

        @pl.when(mm < m)
        def _(mm=mm):
            arrived(t_recv.at[mm], t_r.at[mm])
            for i in range(2):
                dd = decay[h * 4 + 2 * c + i]
                gone = (m - 1 - mm).astype(F32) * (2.0 * TOK)
                p_all[2 * c + i] += (
                    jnp.exp(jnp.full((HEAD, HEAD), -dd * gone, F32)) * t_recv[mm, i].astype(F32)
                )

    half_p = p_all.at[pl.ds(2 * c, 2)]
    across = send(half_p, half_p, sp_s.at[1], sp_r.at[1], to_core, False)
    arrived(p_all.at[pl.ds(2 * (1 - c), 2)], sp_r.at[1])

    order = (z_far, z_up, z_dn, z)

    def finish(to, lo, j):
        first = lo + order[j] * 64
        span, out = pl.ds(pl.multiple_of(first, 64), 64), pl.ds(j * 64, 64)
        for i in range(4):
            ahead = (rows_of((64, HEAD)) + (first + 1)).astype(F32)
            lq = qkv[0, span, head_of(i)].astype(F32) * jnp.exp(-rate[i] * ahead)
            full = intra[span, head_of(i)] + jnp.dot(
                lq, p_all[i], preferred_element_type=F32, precision=lax.Precision.HIGHEST
            )
            scale = lax.rsqrt(jnp.mean(full * full, axis=-1, keepdims=True) + EPS)
            to[out, head_of(i)] = (full * scale * lgain[:, head_of(i)]).astype(BF16)

    def four(j):
        return pl.ds(j * 64, 64)

    across.wait_send()

    @pl.when(c == 1)
    def _():
        for i in range(4):
            fade = jnp.exp(jnp.full((HEAD, HEAD), -rate[i] * TOK, F32))
            p_all[i] = fade * p_all[i] + s_pair[i]

    for j in range(4):
        finish(nsend, (1 - xl) * 256, j)
        send(nsend.at[four(j)], nrecv.at[four(j)], n_s.at[j], n_r.at[j], to_pair)
    push(0, 6, 0)
    push(0, 7, 0)
    for k in range(4):
        push(1, k, 0)
        push(2, k, 0)
    relay(0, 2)
    for j in range(4):
        finish(nown, xl * 256, j)
    mirror(0, 0)
    relay(0, 3)
    own[0].wait()

    def project(k, lo, count):
        at, rows = pl.ds(k * CH, CH), pl.ds(lo, count)
        total = dot(nown[rows, :], wo_own[:, at]) + dot(nrecv[rows, :], wo_par[:, at])
        part[rows, at] = total.astype(BF16)

    def far(k):
        ready(0, k)
        project(k, 0, 64)
        left, right = pl.ds(k * CH, HALF), pl.ds(k * CH + HALF, HALF)
        slot = pl.ds(k * HALF, HALF)
        send(part.at[four(0), left], a_p.at[:, slot], a_s.at[k, 0], a_r.at[k, 0], to_zu)
        send(part.at[four(0), right], a_m.at[:, slot], a_s.at[k, 1], a_r.at[k, 1], to_zd)

    def join(k):
        left, right = pl.ds(k * CH, HALF), pl.ds(k * CH + HALF, HALF)
        slot, chunk = pl.ds(k * HALF, HALF), pl.ds(k * CH, CH)
        project(k, 64, 192)
        arrived(a_p.at[:, slot], a_r.at[k, 0])
        part[four(1), left] = (
            part[four(1), left].astype(F32) + a_p[:, slot].astype(F32)
        ).astype(BF16)
        send(part.at[four(1), chunk], b_p.at[:, chunk], b_s.at[k, 0], b_r.at[k, 0], to_zu)
        arrived(a_m.at[:, slot], a_r.at[k, 1])
        part[four(2), right] = (
            part[four(2), right].astype(F32) + a_m[:, slot].astype(F32)
        ).astype(BF16)
        send(part.at[four(2), chunk], b_m.at[:, chunk], b_s.at[k, 1], b_r.at[k, 1], to_zd)

    def close(k):
        chunk = pl.ds(k * CH, CH)
        arrived(b_p.at[:, chunk], b_r.at[k, 0])
        arrived(b_m.at[:, chunk], b_r.at[k, 1])
        total = (
            residual[:, chunk].astype(F32) + part[four(3), chunk].astype(F32)
            + b_p[:, chunk].astype(F32) + b_m[:, chunk].astype(F32)
        )
        upd[:, chunk] = total
        return jnp.sum(total * total, axis=-1, keepdims=True)

    arrived(nrecv.at[four(0)], n_r.at[0])
    far(0)
    mirror(0, 1)
    far(1)
    relay(0, 4)
    for j in range(1, 4):
        arrived(nrecv.at[four(j)], n_r.at[j])
    join(0)
    mirror(0, 2)
    far(2)
    relay(0, 5)
    join(1)
    mirror(0, 3)
    far(3)
    relay(0, 6)
    join(2)
    mirror(0, 4)
    far(4)
    relay(0, 7)
    join(3)
    mirror(0, 5)
    far(5)
    join(4)
    mirror(0, 6)
    far(6)
    join(5)
    mirror(0, 7)
    far(7)
    join(6)
    join(7)
    kvbuf[:, :, :, pl.ds(256, HEAD)] = jnp.ones((24, NP, R, HEAD), BF16)
    own[2].wait()
    separate(wkv_own, wq_own, 0, MODEL)
    relay(1, 0)
    relay(2, 0)
    square = close(0)
    for k in range(1, 4):
        square += close(k)
    relay(1, 1)
    relay(2, 1)
    square += close(4)
    square += close(5)
    mirror(1, 0)
    mirror(2, 0)
    square += close(6)
    square += close(7)
    scale = lax.rsqrt(square * (1.0 / MODEL) + EPS)
    store = pltpu.make_async_copy(upd, upd_out, own_sem.at[3])
    store.start()

    for p in range(NP):
        row = pl.ds(p * R, R)
        gath[p, z] = (upd[row, :] * scale[p * R : (p + 1) * R] * again[...]).astype(BF16)
        mine = gath.at[p, z]
        send(mine, mine, g_s.at[p, 0], g_r.at[p, 0], to_zu)
        send(mine, mine, g_s.at[p, 1], g_r.at[p, 1], to_zd)

    def forward(p):
        below, above = gath.at[p, z_dn], gath.at[p, z_up]
        left, right = pl.ds(0, MODEL // 2), pl.ds(MODEL // 2, MODEL // 2)
        arrived(below, g_r.at[p, 0])
        send(below.at[:, left], below.at[:, left], g_s.at[p, 2], g_r.at[p, 2], to_zu)
        arrived(above, g_r.at[p, 1])
        send(above.at[:, right], above.at[:, right], g_s.at[p, 3], g_r.at[p, 3], to_zd)

    def gathered(p):
        far = gath.at[p, z_far]
        arrived(far.at[:, pl.ds(0, MODEL // 2)], g_r.at[p, 2])
        arrived(far.at[:, pl.ds(MODEL // 2, MODEL // 2)], g_r.at[p, 3])

    kv = pl.ds(0, 256)
    mine_half, mine_kv = pl.ds(xl * 4, 4), pl.ds(16 + xl * 4, 4)

    def second(p):
        acc[...] = jnp.zeros_like(acc)

        def deep(j, carry):
            at = pl.ds(pl.multiple_of(j * 1024, 1024), 1024)
            lhs = gath[p, :, :, at].reshape(4 * R, 1024)
            acc[:, pl.ds(0, QKV)] += dot(lhs, wq_own[at, :])
            acc[:, pl.ds(QKV, QKV)] += dot(lhs, wq_par[at, :])
            return carry

        lax.fori_loop(0, 6, deep, 0)
        stkv[p] = acc[:, pl.ds(QKV + 512, 256)].astype(BF16).reshape(4, R, 256)
        kvbuf[mine_kv, p, :, kv] = acc[:, pl.ds(512, 256)].astype(BF16).reshape(4, R, 256)
        send(stkv.at[p], kvbuf.at[mine_kv, p, :, kv], x_s.at[p, 0], x_r.at[p, 0], to_pair)
        for step in (1, 2):

            @pl.when(s + step < 16)
            def _(step=step):
                slot = kvbuf.at[pl.ds(16 - 8 * step + xl * 4, 4), p, :, kv]
                sem = h_r.at[p, step - 1, xl]
                send(kvbuf.at[mine_kv, p, :, kv], slot, h_s.at[p, step - 1, 0], sem, (s + step, h), False)
                send(stkv.at[p], slot, h_s.at[p, step - 1, 1], sem, (s + step, other), False)

        stq[p] = acc[:, pl.ds(QKV, 512)].astype(BF16).reshape(4, R, 512)
        send(stq.at[p], qbuf.at[mine_half, p], x_s.at[p, 1], x_r.at[p, 1], to_pair)
        qbuf[mine_half, p] = acc[:, pl.ds(0, 512)].astype(BF16).reshape(4, R, 512)

    for k in (2, 3):
        relay(1, k)
        relay(2, k)
        mirror(1, k - 1)
        mirror(2, k - 1)
    forward(0)
    mirror(1, 3)
    mirror(2, 3)
    forward(1)
    for k in range(4):
        separate(wkv_par, wq_par, c * 3072 + k * 768, 768)
    own[1].wait()
    for k in range(4):
        ready(1, k)
        ready(2, k)
        separate(wkv_par, wq_par, (1 - c) * 3072 + k * 768, 768)
    gathered(0)
    second(0)
    gathered(1)
    second(1)

    @pl.when(s < 1)
    def _():
        kvbuf[pl.ds(8, 8), :, :, kv] = jnp.zeros((8, NP, R, 256), BF16)

    @pl.when(s < 2)
    def _():
        kvbuf[pl.ds(0, 8), :, :, kv] = jnp.zeros((8, NP, R, 256), BF16)

    for p in range(NP):
        arrived(kvbuf.at[pl.ds(16 + (1 - xl) * 4, 4), p, :, kv], x_r.at[p, 0])
        for step in (1, 2):

            @pl.when(s - step >= 0)
            def _(p=p, step=step):
                for hf in (0, 1):
                    slot = kvbuf.at[pl.ds(16 - 8 * step + hf * 4, 4), p, :, kv]
                    arrived(slot, h_r.at[p, step - 1, hf])

        arrived(qbuf.at[pl.ds((1 - xl) * 4, 4), p], x_r.at[p, 1])

    factor = HEAD**-0.5 * 1.4426950408889634

    def attend(t, carry):
        row, col = rows_of((HEAD, 1)), cols_of((HEAD, 640))
        early = 1024 - s * TOK - t * HEAD
        middle = cols_of((HEAD, 384)) + 640 >= early
        last = cols_of((HEAD, HEAD)) <= row
        keys = kvbuf[pl.ds(2 * t, 18), :, :, pl.ds(0, HEAD)].reshape(1152, HEAD)
        vals = kvbuf[pl.ds(2 * t, 18), :, :, pl.ds(HEAD, 256)].reshape(1152, 256)
        for i in range(4):
            first = jnp.maximum(row + (1025 - window[h * 4 + i]), early)
            q = qbuf[pl.ds(2 * t, 2), :, :, head_of(i)].reshape(HEAD, HEAD)
            sc = dot_t(q, keys)
            sc = jnp.concatenate(
                (
                    jnp.where(col >= first, sc[:, :640], -1e30),
                    jnp.where(middle, sc[:, 640:1024], -1e30),
                    jnp.where(last, sc[:, 1024:], -1e30),
                ),
                axis=1,
            )
            top = jnp.max(sc, axis=-1, keepdims=True)
            pr = jnp.exp2((sc - top) * factor).astype(BF16)
            both = dot(pr, vals)
            out = both[:, :HEAD] / both[:, HEAD:]
            att_out[pl.ds(pl.multiple_of(t * HEAD, HEAD), HEAD), head_of(i)] = out.astype(BF16)
        return carry

    lax.fori_loop(0, 4, attend, 0)

    store.wait()
    for cp in sent:
        cp.wait_send()
    for mm in range(1, 8):

        @pl.when(m < mm)
        def _(mm=mm):
            pltpu.make_async_copy(t_send, t_send, t_s.at[mm - 1]).wait()

    for p in range(NP):
        for step in (1, 2):

            @pl.when(s + step < 16)
            def _(p=p, step=step):
                pltpu.make_async_copy(stkv.at[p], stkv.at[p], h_s.at[p, step - 1, 0]).wait()
                pltpu.make_async_copy(stkv.at[p], stkv.at[p], h_s.at[p, step - 1, 1]).wait()


def on_device(
    lightning_qkv,
    residual,
    decay_rate,
    lightning_gain,
    out_weight,
    attn_gain,
    query_weight,
    key_value_weight,
    window,
):
    vmem = pl.BlockSpec(memory_space=pltpu.VMEM)
    smem = pl.BlockSpec(memory_space=pltpu.SMEM)
    anyw = pl.BlockSpec(memory_space=pl.ANY)
    dma = pltpu.SemaphoreType.DMA
    V = pltpu.VMEM
    return pl.pallas_call(
        body,
        out_shape=(
            jax.ShapeDtypeStruct((64, MODEL), F32),
            jax.ShapeDtypeStruct((TOK, 512), BF16),
        ),
        in_specs=[vmem, vmem, smem, vmem, anyw, vmem, anyw, anyw, smem],
        out_specs=(anyw, vmem),
        scratch_shapes=[
            V((512, MODEL), BF16),
            V((512, MODEL), BF16),
            V((MODEL, QKV), BF16),
            V((MODEL, QKV), BF16),
            V((2 * MODEL, HEAD), BF16),
            V((2 * MODEL, HEAD), BF16),
            V((768, HEAD), F32),
            V((4, HEAD, HEAD), F32),
            V((4, HEAD, HEAD), F32),
            V((2, HEAD, HEAD), BF16),
            V((7, 2, HEAD, HEAD), BF16),
            V((4, HEAD, HEAD), F32),
            V((TOK, 512), F32),
            V((256, 512), BF16),
            V((256, 512), BF16),
            V((256, 512), BF16),
            V((256, MODEL), BF16),
            V((64, MODEL // 2), BF16),
            V((64, MODEL // 2), BF16),
            V((64, MODEL), BF16),
            V((64, MODEL), BF16),
            V((64, MODEL), F32),
            V((NP, 4, R, MODEL), BF16),
            V((4 * R, 2 * QKV), F32),
            V((8, NP, R, 512), BF16),
            V((24, NP, R, 384), BF16),
            V((NP, 4, R, 512), BF16),
            V((NP, 4, R, 256), BF16),
            dma((4,)),
            dma((3, NCH, 5)),
            dma((3, NCH, 5)),
            dma((2,)),
            dma((2,)),
            dma((7,)),
            dma((7,)),
            dma((4,)),
            dma((4,)),
            dma((NCH, 2)),
            dma((NCH, 2)),
            dma((NCH, 2)),
            dma((NCH, 2)),
            dma((NP, 4)),
            dma((NP, 4)),
            dma((NP, 2)),
            dma((NP, 2)),
            dma((NP, 2, 2)),
            dma((NP, 2, 2)),
        ],
        compiler_params=pltpu.CompilerParams(
            collective_id=0, has_side_effects=True, vmem_limit_bytes=60 * 2**20
        ),
    )(
        jnp.transpose(lightning_qkv, (1, 0, 2)),
        residual,
        decay_rate,
        lightning_gain.reshape(1, 512),
        out_weight,
        attn_gain.reshape(1, MODEL),
        query_weight,
        key_value_weight.reshape(2 * MODEL, HEAD),
        window,
    )


def solution(mesh):
    placed = (
        P("seq", None, "head"),
        P(("seq", "head"), None),
        P(),
        P("head"),
        P("head", None),
        P(),
        P(None, "head"),
        P(None, "head", None, None),
        P(),
    )
    return jax.shard_map(
        on_device,
        mesh=mesh,
        in_specs=placed,
        out_specs=(P(("seq", "head"), None), P("seq", "head")),
        check_vma=False,
    )
```
